32 devices in a mesh: groups: 2 (over y), feat: 4 (over z), tm: 2 (over x), sub: 2 (over core).
Axes of the slice: x: 2, y: 2, z: 4, core: 2. Of those that a mesh axis runs over, the one named last changes fastest.
Arguments:
- frames: bfloat16 [8, 256, 8192], P('groups', 'tm', ('feat', 'sub')), parts along dimension 0, may hold values from -16 to 19
- window_starts: int32 [8], P('groups'), parts along dimension 0, may hold values from 0 to 32, as said below
- lag_frames: int32 [8], P('groups'), parts along dimension 0, may hold values from 1 to 64
Outputs:
- covariance_zero: float32 [16384, 8192], P(('groups', 'feat'), ('tm', 'sub')), parts along dimension 0
- covariance_lag: float32 [16384, 8192], P(('groups', 'feat'), ('tm', 'sub')), parts along dimension 0
The draws below stay inside these ranges and needn't reach their ends.
There are 2 independent parts, one for each index of `groups`. The reference program is written for one: setup_inputs(seed, part) draws one part's arguments, and reference() takes and returns one part's arrays. A program takes and returns all parts, laid end to end along the dimension named above; each array names one. Nothing has to cross between parts.
Inputs may be any that keep to these rules, and one draw needn't show every extreme that they name: `window_starts`: first frame of each trajectory's window.
All inputs are finite; a program needn't handle non-finite values.
Results may differ from the reference program's by a relative error of at most 0.0003.
Values may be sent and summed in bfloat16 or wider, within the bound.
No kernel may reach another device: no remote copies, remote signals or barrier semaphores. Data moves between devices by JAX's collectives and lax.ppermute only.
A program may use at most 128 MiB of HBM per device.

```python
import math
import jax
import jax.numpy as jnp
from jax import lax

F = 8192
TRAJ = 4
STORE = 256
SLACK = 32
LAGMAX = 64
WIN = 224


def draw_frames(key, part):
    key = jax.random.fold_in(key, 5)
    subkeys = jax.random.split(key, 6)
    spread = jnp.exp(jax.random.uniform(subkeys[0], (F,), jnp.float32, math.log(0.4), math.log(1.6)))
    jitter = jax.random.truncated_normal(subkeys[5], -4.0, 4.0, (TRAJ, STORE, F), jnp.float32)
    offset = jax.random.uniform(subkeys[1], (F,), jnp.float32, 0.5, 2.5)
    amplitude = jax.random.uniform(subkeys[2], (TRAJ, 1, F), jnp.float32, 0.3, 1.5)
    frequency = jnp.exp(jax.random.uniform(subkeys[3], (TRAJ, 1, F), jnp.float32, math.log(0.3), math.log(3.0))) / LAGMAX
    phases = jax.random.uniform(subkeys[4], (TRAJ, 1, F), jnp.float32, -math.pi, math.pi)
    instant = jnp.arange(STORE, dtype=jnp.float32)[None, :, None]
    values = offset + spread * (jitter + amplitude * jnp.cos(frequency * instant + phases))
    return values.astype(jnp.bfloat16)


def draw_window_starts(key, part):
    key = jax.random.fold_in(key, 17)
    subkeys = jax.random.split(key, 2)
    values = jax.random.randint(subkeys[0], (TRAJ,), 0, SLACK + 1)
    chosen = jax.random.randint(subkeys[1], (), 0, TRAJ)
    return jnp.where(jnp.arange(TRAJ) == chosen, SLACK, values).astype(jnp.int32)


def draw_lag_frames(key, part):
    key = jax.random.fold_in(key, 29)
    subkeys = jax.random.split(key, 2)
    values = jax.random.randint(subkeys[0], (TRAJ,), 1, LAGMAX + 1)
    chosen = jax.random.randint(subkeys[1], (), 0, TRAJ)
    return jnp.where(jnp.arange(TRAJ) == chosen, LAGMAX, values).astype(jnp.int32)


def setup_inputs(seed: int = 0, part: int = 0) -> dict:
    keys = jax.random.split(jax.random.key(seed), 4)
    part_keys = jax.random.split(jax.random.fold_in(keys[3], part), 4)
    return {
        "frames": draw_frames(jax.random.fold_in(jax.random.fold_in(keys[3], part), 71), part),
        "window_starts": draw_window_starts(jax.random.fold_in(jax.random.fold_in(keys[3], part), 71), part),
        "lag_frames": draw_lag_frames(jax.random.fold_in(jax.random.fold_in(keys[3], part), 71), part),
    }


def window_masks(window_starts, lag_frames, stored):
    instant = jnp.arange(stored, dtype=jnp.int32)[None, :]
    window_begin = window_starts[:, None]
    shift_by = lag_frames[:, None]
    finish = window_begin + (stored - SLACK)
    base_mask = (instant >= window_begin) & (instant < finish - shift_by)
    lag_mask = (instant >= window_begin + shift_by) & (instant < finish)
    return base_mask.astype(jnp.bfloat16), lag_mask.astype(jnp.bfloat16)


def shift_ahead(series, lag_frames):
    stored = series.shape[1]
    padded = jnp.pad(series, ((0, 0), (0, LAGMAX), (0, 0)))

    def one_series(padded_rows, shift_by):
        return lax.dynamic_slice_in_dim(padded_rows, shift_by.astype(jnp.int32), stored, 0)

    return jax.vmap(one_series)(padded, lag_frames)


def reference(frames, window_starts, lag_frames):
    stored = frames.shape[1]
    base_mask, lag_mask = window_masks(window_starts, lag_frames, stored)
    frame_count = (TRAJ * WIN - jnp.sum(lag_frames)).astype(jnp.float32)
    wide = frames.astype(jnp.float32)
    base_wide = base_mask.astype(jnp.float32)
    zero_mean = jnp.einsum("kt,ktf->f", base_wide, wide) / frame_count
    later_mean = jnp.einsum("kt,ktf->f", lag_mask.astype(jnp.float32), wide) / frame_count
    masked = (wide * base_wide[:, :, None]).reshape(-1, F)
    ahead = shift_ahead(frames, lag_frames).astype(jnp.float32).reshape(-1, F)
    flat = wide.reshape(-1, F)
    zero_sum = jnp.dot(masked.T, flat, preferred_element_type=jnp.float32, precision=lax.Precision.HIGHEST)
    covariance_zero = zero_sum / frame_count - zero_mean[:, None] * zero_mean[None, :]
    lag_sum = jnp.dot(masked.T, ahead, preferred_element_type=jnp.float32, precision=lax.Precision.HIGHEST)
    covariance_lag = lag_sum / frame_count - zero_mean[:, None] * later_mean[None, :]
    return covariance_zero, covariance_lag
```

```python
import functools

import jax
import jax.numpy as jnp
from jax import lax
from jax.experimental import pallas as pl
from jax.experimental.pallas import tpu as pltpu
from jax.sharding import PartitionSpec as P

SLACK = 32
LAGMAX = 64
AXES = ("feat", "tm", "sub")
VMEM_LIMIT = 48 * 1024 * 1024


def spread(x, axis, root):
    mine = lax.axis_index(axis) == root
    return lax.psum(jnp.where(mine, x, jnp.zeros_like(x)), axis)


def window_masks(window_starts, lag_frames, stored):
    instant = jnp.arange(stored, dtype=jnp.int32)[None, :]
    window_begin = window_starts[:, None]
    shift_by = lag_frames[:, None]
    finish = window_begin + (stored - SLACK)
    base_mask = (instant >= window_begin) & (instant < finish - shift_by)
    lag_mask = (instant >= window_begin + shift_by) & (instant < finish)
    return (base_mask.astype(jnp.bfloat16), lag_mask.astype(jnp.bfloat16))


def shift_ahead(series, lag_frames):
    stored = series.shape[1]
    padded = jnp.pad(series, ((0, 0), (0, LAGMAX), (0, 0)))

    def one_series(padded_rows, shift_by):
        return lax.dynamic_slice_in_dim(padded_rows, shift_by, stored, 0)

    return jax.vmap(one_series)(padded, lag_frames)


def frame_product(left, right):
    return lax.dot_general(
        left, right, (((0, 1), (0, 1)), ((), ())), preferred_element_type=jnp.float32
    )


def frame_mean(mask, series, frame_count):
    return jnp.einsum("kt,ktf->f", mask, series, preferred_element_type=jnp.float32) / frame_count


def general(frames, window_starts, lag_frames):
    halves = lax.all_gather(frames, "sub", axis=2, tiled=True)
    row_data = lax.all_gather(halves, "tm", axis=1, tiled=True)
    stored = row_data.shape[1]
    base_mask, lag_mask = window_masks(window_starts, lag_frames, stored)
    frame_count = (row_data.shape[0] * (stored - SLACK) - jnp.sum(lag_frames)).astype(jnp.float32)
    masked_rows = row_data * base_mask[:, :, None]
    row_mean = frame_mean(base_mask, row_data, frame_count)
    groups = lax.axis_size("tm") * lax.axis_size("sub")
    per_group = lax.axis_size("feat") // groups
    column = lax.axis_index("tm") * lax.axis_size("sub") + lax.axis_index("sub")
    tile_parts = []
    for member in range(per_group):
        column_block = spread(row_data, "feat", column * per_group + member)
        zero_mean = frame_mean(base_mask, column_block, frame_count)
        later_mean = frame_mean(lag_mask, column_block, frame_count)
        zero_part = (
            frame_product(masked_rows, column_block) / frame_count
            - row_mean[:, None] * zero_mean[None, :]
        )
        crossed = frame_product(masked_rows, shift_ahead(column_block, lag_frames))
        lag_part = crossed / frame_count - row_mean[:, None] * later_mean[None, :]
        tile_parts.append((zero_part, lag_part))
    covariance_zero = jnp.concatenate([entries[0] for entries in tile_parts], axis=1)
    covariance_lag = jnp.concatenate([entries[1] for entries in tile_parts], axis=1)
    return (covariance_zero, covariance_lag)


def rank(z, x, c):
    return (z * 2 + x) * 2 + c


def hops(links):
    pairs = []
    for x, src, dst in links:
        for c in range(2):
            pairs.append((rank(src, x, c), rank(dst, x, c)))
            pairs.append((rank(3 - src, 1 - x, c), rank(3 - dst, 1 - x, c)))
    return pairs


def crossings(where):
    return [(rank(z, x, c), rank(z, 1 - x, c)) for z, x in where for c in range(2)]


CORES = [(rank(z, x, c), rank(z, x, 1 - c)) for z in range(4) for x in range(2) for c in range(2)]
PLANES = crossings([(z, x) for z in range(4) for x in range(2)])
NEXT = hops([(0, 0, 1), (0, 1, 2), (0, 2, 3)])
FAR = hops([(1, 0, 1), (1, 1, 3)])
FAR_AGAIN = hops([(1, 1, 3)])
ENDS = crossings([(0, 0), (0, 1), (3, 0), (3, 1)])
LAST = hops([(0, 1, 2), (0, 2, 3)])
BACK = hops([(1, 2, 3), (0, 3, 2)])
LAST_CROSS = crossings([(3, 1), (0, 0)])


def send(x, pairs):
    return lax.ppermute(x, AXES, pairs)


def rows_kernel(
    count_ref, starts_ref, lags_ref, x_ref, own_ref, other_ref, zero_ref, late_ref, sum_ref, *, window
):
    trajectories, half = own_ref.shape[0], own_ref.shape[1]
    stored = 2 * half
    first = x_ref[0] == 0
    instant = lax.broadcasted_iota(jnp.int32, (stored, 1), 0)
    total = jnp.zeros((own_ref.shape[2], half), jnp.float32)
    for k in range(trajectories):
        own = own_ref[k].astype(jnp.float32)
        other = other_ref[k].astype(jnp.float32)
        series = jnp.concatenate(
            [jnp.where(first, own, other), jnp.where(first, other, own)], axis=0
        )
        start, lag = starts_ref[k], lags_ref[k]
        kept = (instant >= start) & (instant < start + window - lag)
        masked = jnp.where(kept, series, 0.0)
        moved = pltpu.roll(masked, lag, axis=0)
        for values, out_ref in ((masked, zero_ref), (moved, late_ref)):
            turned = values.T
            low, high = turned[:, :half], turned[:, half:]
            mine = jnp.where(first, low, high)
            theirs = jnp.where(first, high, low)
            out_ref[:, k * half : (k + 1) * half] = mine.astype(jnp.bfloat16)
            out_ref[:, (trajectories + k) * half : (trajectories + k + 1) * half] = theirs.astype(
                jnp.bfloat16
            )
            if out_ref is zero_ref:
                total = total + mine + theirs
    mean = jnp.sum(total, axis=1, keepdims=True) / count_ref[0]
    sum_ref[...] = jnp.broadcast_to(mean, sum_ref.shape)


def prepare_rows(scalars, place, own, other, before, window):
    trajectories, half, features = own.shape
    tile = 256
    depth = trajectories * 2 * half
    count, starts, lags, x = scalars
    steps = features // tile
    out_shape = (
        jax.ShapeDtypeStruct((2 * features, depth), jnp.bfloat16),
        jax.ShapeDtypeStruct((2 * features, depth), jnp.bfloat16),
        jax.ShapeDtypeStruct((2 * features, 128), jnp.float32),
    )

    def spot(i, place_ref, *_):
        return (place_ref[0] * steps + i, 0)

    data = pl.BlockSpec((trajectories, half, tile), lambda i, *_: (0, 0, i))
    outs = [pl.BlockSpec((tile, depth), spot)] * 2 + [pl.BlockSpec((tile, 128), spot)]

    def body(place_ref, count_ref, starts_ref, lags_ref, x_ref, own_ref, other_ref, *refs):
        rows_kernel(
            count_ref, starts_ref, lags_ref, x_ref, own_ref, other_ref, *refs[-3:], window=window
        )

    return pl.pallas_call(
        body,
        out_shape=out_shape,
        grid_spec=pltpu.PrefetchScalarGridSpec(
            num_scalar_prefetch=5,
            grid=(steps,),
            in_specs=[data, data] + [pl.BlockSpec(memory_space=pl.ANY)] * len(before),
            out_specs=outs,
        ),
        input_output_aliases={7 + i: i for i in range(len(before))},
        compiler_params=pltpu.CompilerParams(vmem_limit_bytes=VMEM_LIMIT),
        cost_estimate=pl.CostEstimate(
            flops=0, bytes_accessed=24 * features * depth, transcendentals=0
        ),
        name="rows",
    )(place, count, starts, lags, x, own, other, *before)


def product_kernel(
    place_ref, count_ref, masks_ref, zero_ref, late_ref, mean_ref, mine_own_ref, mine_other_ref,
    sib_ref, *refs
):
    cov_zero_ref, cov_late_ref, means_ref = refs[-3:]
    i, j = pl.program_id(0), pl.program_id(1)
    depth = mine_own_ref.shape[0]
    scale = 1.0 / count_ref[0]

    def dot(left, right):
        return jnp.dot(left, right, preferred_element_type=jnp.float32)

    def strip(own, other):
        @pl.when(i == 0)
        def _():
            sums = dot(masks_ref[:, :depth], own) + dot(masks_ref[:, depth:], other)
            means_ref[j] = sums * scale

        row_mean = mean_ref[:, :1]
        for left_ref, out_ref, which in ((zero_ref, cov_zero_ref, 0), (late_ref, cov_late_ref, 8)):
            total = dot(left_ref[:, :depth], own) + dot(left_ref[:, depth:], other)
            out_ref[...] = total * scale - row_mean * means_ref[j, which : which + 1, :]

    @pl.when(j == 0)
    def _():
        strip(mine_own_ref[...], mine_other_ref[...])

    @pl.when(j == 1)
    def _():
        strip(sib_ref[0], sib_ref[1])


def product(place, count, masks, rows, mine_own, mine_other, sib, first, before, features):
    zero, late, means = rows
    height, depth = zero.shape
    width = mine_own.shape[-1]
    tile = min(512, height)
    half = depth // 2
    out = jax.ShapeDtypeStruct((height, 2 * features), jnp.float32)
    strips = features // width

    def spot(i, j, place_ref, *_):
        part = jnp.where(j == 0, place_ref[0], 1 - place_ref[0])
        return (i, part * strips + first // width)

    left = pl.BlockSpec((tile, depth), lambda i, j, *_: (i, 0))
    piece = pl.BlockSpec((half, width), lambda i, j, *_: (0, 0))
    return pl.pallas_call(
        product_kernel,
        out_shape=(out, out),
        grid_spec=pltpu.PrefetchScalarGridSpec(
            num_scalar_prefetch=2,
            grid=(height // tile, 2),
            in_specs=[
                pl.BlockSpec((16, depth), lambda i, j, *_: (0, 0)),
                left,
                left,
                pl.BlockSpec((tile, 128), lambda i, j, *_: (i, 0)),
                piece,
                piece,
                pl.BlockSpec((2, half, width), lambda i, j, *_: (0, 0, 0)),
            ]
            + [pl.BlockSpec(memory_space=pl.ANY)] * len(before),
            out_specs=[pl.BlockSpec((tile, width), spot)] * 2,
            scratch_shapes=[pltpu.VMEM((2, 16, width), jnp.float32)],
        ),
        input_output_aliases={9 + i: i for i in range(len(before))},
        compiler_params=pltpu.CompilerParams(vmem_limit_bytes=VMEM_LIMIT),
        cost_estimate=pl.CostEstimate(
            flops=8 * height * depth * width,
            bytes_accessed=4 * height * depth + 16 * height * width,
            transcendentals=0,
        ),
        name="covariances",
    )(place, count, masks, zero, late, means, mine_own, mine_other, sib, *before)


def chunk_sizes(features):
    return [features // 2, features // 2]


def line_of_four(frames, window_starts, lag_frames):
    trajectories, half, features = frames.shape
    stored = 2 * half
    window = stored - SLACK
    z, x, c = (lax.axis_index(a) for a in AXES)
    zm = jnp.where(x == 1, 3 - z, z)
    far_mine = c == x
    count = (trajectories * window - jnp.sum(lag_frames)).astype(jnp.float32).reshape(1)
    plane = x.astype(jnp.int32).reshape(1)
    scalars = (count, window_starts, lag_frames, plane)
    place = c.astype(jnp.int32).reshape(1)

    own = frames
    cross = send(own, PLANES)
    near1 = send(own, NEXT)
    far1 = send(own, FAR)
    sib_own = send(own, CORES)

    near2 = send(jnp.where(zm == 0, cross, near1), NEXT)
    far2 = send(far1, FAR_AGAIN)
    ends = send(jnp.where(zm == 0, far1, near1), ENDS)
    sib_cross = send(cross, CORES)

    rows = prepare_rows(scalars, place, own, cross, (), window)
    rows = prepare_rows(scalars, 1 - place, sib_own, sib_cross, rows, window)

    base_mask, lag_mask = window_masks(window_starts, lag_frames, stored)

    def relative(mask):
        low, high = mask[:, :half].reshape(-1), mask[:, half:].reshape(-1)
        return jnp.where(x == 0, jnp.concatenate([low, high]), jnp.concatenate([high, low]))

    masks = jnp.concatenate(
        [
            jnp.broadcast_to(relative(m)[None, :], (8, trajectories * stored))
            for m in (base_mask, lag_mask)
        ]
    )

    outs = ()
    first = 0
    for width in chunk_sizes(features):
        part = lambda a: a[:, :, first : first + width]
        own_p, cross_p, near1_p, near2_p, far2_p, ends_p = (
            part(a) for a in (own, cross, near1, near2, far2, ends)
        )
        near3 = send(near2_p, LAST)
        back = send(jnp.where(zm == 1, own_p, ends_p), BACK)
        cross3 = send(far2_p, LAST_CROSS)
        far_own = lax.select_n(zm, own_p, near1_p, near2_p, near3)
        far_other = lax.select_n(zm, cross_p, near2_p, near3, cross3)
        close_own = lax.select_n(zm, back, own_p, near1_p, near2_p)
        close_other = lax.select_n(zm, ends_p, cross_p, back, ends_p)
        mine_own = jnp.where(far_mine, far_own, close_own)
        mine_other = jnp.where(far_mine, far_other, close_other)
        give_own = jnp.where(far_mine, close_own, far_own)
        give_other = jnp.where(far_mine, close_other, far_other)
        sib = send(jnp.stack([give_own, give_other]), CORES)
        flat = lambda a: a.reshape(a.shape[:-3] + (trajectories * half, width))
        outs = product(
            place, count, masks, rows, flat(mine_own), flat(mine_other), flat(sib), first, outs, features
        )
        first += width
    return outs


def solution(mesh):
    placed = (P("groups", "tm", ("feat", "sub")), P("groups"), P("groups"))
    line = mesh.shape["feat"] == 4 and mesh.shape["tm"] == 2 and mesh.shape["sub"] == 2
    return jax.shard_map(
        line_of_four if line else general,
        mesh=mesh,
        in_specs=placed,
        out_specs=(P(("groups", "feat"), ("tm", "sub")), P(("groups", "feat"), ("tm", "sub"))),
        check_vma=False,
    )
```

```python
import functools

import jax
import jax.numpy as jnp
from jax import lax
from jax.experimental import pallas as pl
from jax.experimental.pallas import tpu as pltpu
from jax.sharding import PartitionSpec as P

SLACK = 32
LAGMAX = 64
AXES = ("feat", "tm", "sub")
VMEM_LIMIT = 60 * 1024 * 1024
TILE = 512
DEPTH = 2
ROWS_TILE = 1024


def spread(x, axis, root):
    mine = lax.axis_index(axis) == root
    return lax.psum(jnp.where(mine, x, jnp.zeros_like(x)), axis)


def window_masks(window_starts, lag_frames, stored):
    instant = jnp.arange(stored, dtype=jnp.int32)[None, :]
    window_begin = window_starts[:, None]
    shift_by = lag_frames[:, None]
    finish = window_begin + (stored - SLACK)
    base_mask = (instant >= window_begin) & (instant < finish - shift_by)
    lag_mask = (instant >= window_begin + shift_by) & (instant < finish)
    return (base_mask.astype(jnp.bfloat16), lag_mask.astype(jnp.bfloat16))


def shift_ahead(series, lag_frames):
    stored = series.shape[1]
    padded = jnp.pad(series, ((0, 0), (0, LAGMAX), (0, 0)))

    def one_series(padded_rows, shift_by):
        return lax.dynamic_slice_in_dim(padded_rows, shift_by, stored, 0)

    return jax.vmap(one_series)(padded, lag_frames)


def frame_product(left, right):
    return lax.dot_general(
        left, right, (((0, 1), (0, 1)), ((), ())), preferred_element_type=jnp.float32
    )


def frame_mean(mask, series, frame_count):
    return jnp.einsum("kt,ktf->f", mask, series, preferred_element_type=jnp.float32) / frame_count


def general(frames, window_starts, lag_frames):
    halves = lax.all_gather(frames, "sub", axis=2, tiled=True)
    row_data = lax.all_gather(halves, "tm", axis=1, tiled=True)
    stored = row_data.shape[1]
    base_mask, lag_mask = window_masks(window_starts, lag_frames, stored)
    frame_count = (row_data.shape[0] * (stored - SLACK) - jnp.sum(lag_frames)).astype(jnp.float32)
    masked_rows = row_data * base_mask[:, :, None]
    row_mean = frame_mean(base_mask, row_data, frame_count)
    groups = lax.axis_size("tm") * lax.axis_size("sub")
    per_group = lax.axis_size("feat") // groups
    column = lax.axis_index("tm") * lax.axis_size("sub") + lax.axis_index("sub")
    tile_parts = []
    for member in range(per_group):
        column_block = spread(row_data, "feat", column * per_group + member)
        zero_mean = frame_mean(base_mask, column_block, frame_count)
        later_mean = frame_mean(lag_mask, column_block, frame_count)
        zero_part = (
            frame_product(masked_rows, column_block) / frame_count
            - row_mean[:, None] * zero_mean[None, :]
        )
        crossed = frame_product(masked_rows, shift_ahead(column_block, lag_frames))
        lag_part = crossed / frame_count - row_mean[:, None] * later_mean[None, :]
        tile_parts.append((zero_part, lag_part))
    covariance_zero = jnp.concatenate([entries[0] for entries in tile_parts], axis=1)
    covariance_lag = jnp.concatenate([entries[1] for entries in tile_parts], axis=1)
    return (covariance_zero, covariance_lag)


def rank(s, x, c):
    return ((3 - s if x else s) * 2 + x) * 2 + c


def home(s, x):
    return (3 - s if x else s) % 2


def hops(links):
    pairs = []
    for s, d, b in links:
        for x in range(2):
            to = rank(d, x, home(b, x)) if d >= 0 else rank(3 - s, 1 - x, home(b, x))
            pairs.append((rank(s, x, home(b, x)), to))
    return pairs


PLACES = [(s, x) for s in range(4) for x in range(2)]
CORES = [(rank(s, x, c), rank(s, x, 1 - c)) for s, x in PLACES for c in range(2)]
FROM_HOME = [(rank(s, x, home(s, x)), rank(s, x, 1 - home(s, x))) for s, x in PLACES]
CROSS_HOME = [(rank(s, x, home(s, x)), rank(3 - s, 1 - x, home(s, x))) for s, x in PLACES]
CROSS_AWAY = [(rank(s, x, 1 - home(s, x)), rank(3 - s, 1 - x, home(s, x))) for s, x in PLACES]
NEAR_1 = hops([(0, 1, 0), (1, 2, 1), (2, 3, 2)])
FAR_1 = hops([(3, 2, 3), (2, 0, 2)])
NEAR_2 = hops([(0, 1, 0), (1, 2, 0), (2, 3, 1), (3, -1, 2)])
FAR_2 = hops([(2, 0, 3), (0, -1, 2)])
NEAR_3 = hops([(1, 2, 0), (2, 3, 0)])
BACK_3 = hops([(1, 0, 1), (3, 2, 1), (0, -1, 3)])


def send(x, pairs):
    return lax.ppermute(x, AXES, pairs)


def after(value, *others):
    return lax.optimization_barrier((value, *others))[0]


def dot(left, right):
    return jnp.dot(left, right, preferred_element_type=jnp.float32)


def rows_kernel(
    starts_ref, lags_ref, x_ref, count_ref, parts, zero_ref, late_ref, mean_ref, moves_ref, *, window
):
    trajectories, half = parts[0][0].shape[0], parts[0][0].shape[1]
    stored = 2 * half
    p, i = pl.program_id(0), pl.program_id(1)

    @pl.when((p == 0) & (i == 0))
    def _():
        def instant(axis):
            n = lax.broadcasted_iota(jnp.int32, (stored, stored), axis)
            return jnp.where(x_ref[0] == 0, n, lax.rem(n + half, stored))

        frame, column = instant(0), instant(1)
        for k in range(trajectories):
            start, lag = starts_ref[k], lags_ref[k]
            kept = (frame >= start) & (frame < start + window - lag)
            for n, ahead in enumerate((0, lag)):
                moves_ref[k, :, n * stored : (n + 1) * stored] = jnp.where(
                    kept & (column == frame + ahead), 1.0, 0.0
                ).astype(jnp.bfloat16)

    def fill(own_ref, cross_refs):
        total = None
        for k in range(trajectories):
            series = jnp.concatenate([own_ref[k], cross_refs[0][k] + cross_refs[1][k]], axis=0)
            moved = lax.dot_general(
                series,
                moves_ref[k],
                (((0,), (0,)), ((), ())),
                preferred_element_type=jnp.float32,
            )
            total = moved[:, :stored] if total is None else total + moved[:, :stored]
            moved = moved.astype(jnp.bfloat16)
            for n, ref in enumerate((zero_ref, late_ref)):
                for side in range(2):
                    to, at = (side * trajectories + k) * half, n * stored + side * half
                    ref[:, to : to + half] = moved[:, at : at + half]
        mean = jnp.sum(total, axis=1, keepdims=True) / count_ref[0]
        mean_ref[...] = jnp.broadcast_to(mean, mean_ref.shape)

    for n, (own_ref, *cross_refs) in enumerate(parts):
        pl.when(p == n)(functools.partial(fill, own_ref, cross_refs))


def prepare_rows(part, starts, lags, x, count, arrays, window):
    trajectories, half, features = arrays[0][0].shape
    tile = min(ROWS_TILE, features)
    steps = features // tile
    depth = trajectories * 2 * half
    row = jax.ShapeDtypeStruct((2 * features, depth), jnp.bfloat16)
    mean = jax.ShapeDtypeStruct((2 * features, 128), jnp.float32)

    def spot(p, i, part_ref, *_):
        return (jnp.where(p == 0, part_ref[0], 1 - part_ref[0]) * steps + i, 0)

    def body(part_ref, starts_ref, lags_ref, x_ref, count_ref, *refs):
        rows_kernel(
            starts_ref, lags_ref, x_ref, count_ref, (refs[:3], refs[3:6]), *refs[6:], window=window
        )

    return pl.pallas_call(
        body,
        out_shape=(row, row, mean),
        grid_spec=pltpu.PrefetchScalarGridSpec(
            num_scalar_prefetch=5,
            grid=(2, steps),
            in_specs=[
                pl.BlockSpec((trajectories, half, tile), lambda p, i, *_: (0, 0, jnp.where(p == 0, i, steps - 1)))
            ]
            * 3
            + [
                pl.BlockSpec((trajectories, half, tile), lambda p, i, *_: (0, 0, jnp.where(p == 0, 0, i)))
            ]
            * 3,
            out_specs=[
                pl.BlockSpec((tile, depth), spot),
                pl.BlockSpec((tile, depth), spot),
                pl.BlockSpec((tile, 128), spot),
            ],
            scratch_shapes=[pltpu.VMEM((trajectories, 2 * half, 4 * half), jnp.bfloat16)],
        ),
        compiler_params=pltpu.CompilerParams(vmem_limit_bytes=VMEM_LIMIT),
        cost_estimate=pl.CostEstimate(
            flops=0, bytes_accessed=28 * arrays[0][0].size, transcendentals=0
        ),
        name="rows",
    )(part, starts, lags, x, count, *arrays[0], *arrays[1])


def product_kernel(part_ref, pick_ref, count_ref, masks_ref, mean_ref, zero_ref, late_ref, *refs, n_pieces):
    pieces = refs[:n_pieces]
    cov_zero_ref, cov_late_ref, left_ref, columns_ref, made_ref, arrived, fetched, stored = refs[-8:]
    half, width = columns_ref.shape[0] // 2, columns_ref.shape[1]
    tile = left_ref.shape[2]
    steps = left_ref.shape[1]
    depth_out = made_ref.shape[0]
    scale = 1.0 / count_ref[0]
    first = pl.multiple_of(part_ref[0] * width, width)

    def piece_copy(piece, side):
        return pltpu.make_async_copy(
            piece, columns_ref.at[pl.ds(side * half, half)], arrived.at[side]
        )

    def left_copy(n, i):
        return pltpu.make_async_copy(
            (zero_ref, late_ref)[n].at[pl.ds(i * tile, tile)], left_ref.at[n, i], fetched.at[n, i]
        )

    def out_copy(n, i):
        slot = lax.rem(i, depth_out)
        return pltpu.make_async_copy(
            made_ref.at[slot, n],
            (cov_zero_ref, cov_late_ref)[n].at[pl.ds(i * tile, tile), pl.ds(first, width)],
            stored.at[slot, n],
        )

    for side in range(2):
        for m, piece in enumerate(pieces):

            @pl.when(pick_ref[side] == m)
            def _():
                piece_copy(piece, side).start()

    def fetch(i):
        for n in range(2):
            left_copy(n, i).start()

    fetch(0)
    for side in range(2):
        piece_copy(pieces[0], side).wait()
    means = dot(masks_ref[...], columns_ref[...]) * scale

    def step(i, carry):
        @pl.when(i + 1 < steps)
        def _():
            fetch(i + 1)

        row_mean = mean_ref[pl.ds(pl.multiple_of(i * tile, tile), tile), :1]
        for n in range(2):
            left_copy(n, i).wait()

            @pl.when(i >= depth_out)
            def _():
                out_copy(n, i - depth_out).wait()

            total = dot(left_ref[n, i], columns_ref[...])
            made_ref[lax.rem(i, depth_out), n] = total * scale - row_mean * means[8 * n : 8 * n + 1]
            out_copy(n, i).start()
        return carry

    lax.fori_loop(0, steps, step, 0)
    for i in range(max(0, steps - depth_out), steps):
        for n in range(2):
            out_copy(n, i).wait()


def product(part, pick, count, masks, rows, pieces, before):
    zero, late, means = rows
    height, depth = zero.shape
    width = pieces[0].shape[-1]
    tile = min(TILE, height)
    steps = height // tile
    out = jax.ShapeDtypeStruct((height, 2 * width), jnp.float32)
    anywhere = pl.BlockSpec(memory_space=pl.ANY)
    return pl.pallas_call(
        functools.partial(product_kernel, n_pieces=len(pieces)),
        out_shape=(out, out),
        grid_spec=pltpu.PrefetchScalarGridSpec(
            num_scalar_prefetch=3,
            grid=(1,),
            in_specs=[
                pl.BlockSpec((16, depth), lambda i, *_: (0, 0)),
                pl.BlockSpec((height, 128), lambda i, *_: (0, 0)),
            ]
            + [anywhere] * (2 + len(pieces) + len(before)),
            out_specs=[anywhere] * 2,
            scratch_shapes=[
                pltpu.VMEM((2, steps, tile, depth), jnp.bfloat16),
                pltpu.VMEM((depth, width), jnp.bfloat16),
                pltpu.VMEM((DEPTH, 2, tile, width), jnp.float32),
                pltpu.SemaphoreType.DMA((2,)),
                pltpu.SemaphoreType.DMA((2, steps)),
                pltpu.SemaphoreType.DMA((DEPTH, 2)),
            ],
        ),
        input_output_aliases={7 + len(pieces) + i: i for i in range(len(before))},
        compiler_params=pltpu.CompilerParams(vmem_limit_bytes=VMEM_LIMIT),
        cost_estimate=pl.CostEstimate(
            flops=4 * height * depth * width,
            bytes_accessed=4 * height * depth + 8 * height * width,
            transcendentals=0,
        ),
        name="covariances",
    )(part, pick, count, masks, means, zero, late, *pieces, *before)


def line_of_four(frames, window_starts, lag_frames):
    trajectories, half, features = frames.shape
    stored = 2 * half
    window = stored - SLACK
    z, x, c = (lax.axis_index(a) for a in AXES)
    s = jnp.where(x == 1, 3 - z, z)
    count = (trajectories * window - jnp.sum(lag_frames)).astype(jnp.float32).reshape(1)
    plane = x.astype(jnp.int32).reshape(1)
    part = c.astype(jnp.int32).reshape(1)

    base_mask, lag_mask = window_masks(window_starts, lag_frames, stored)

    def relative(mask):
        low, high = mask[:, :half].reshape(-1), mask[:, half:].reshape(-1)
        return jnp.where(x == 0, jnp.concatenate([low, high]), jnp.concatenate([high, low]))

    masks = jnp.concatenate(
        [
            jnp.broadcast_to(relative(m)[None, :], (8, trajectories * stored))
            for m in (base_mask, lag_mask)
        ]
    )

    picks = jnp.array([[[0, 2, 3, 4], [1, 3, 4, 5]], [[5, 0, 2, 3], [3, 1, 5, 6]]], jnp.int32)
    pick = picks[jnp.where(c == x, 0, 1), :, s]

    own = frames
    cross_a = send(own, CROSS_HOME)
    near1_a, far1_a = send(own, NEAR_1), send(own, FAR_1)
    sib = send(own, CORES)
    sib_b = sib
    near1_b, far1_b = send(sib_b, NEAR_1), send(sib_b, FAR_1)
    cross_b = send(after(own, cross_a), CROSS_AWAY)
    near2_a, far2_a = send(jnp.where(s == 0, cross_a, near1_a), NEAR_2), send(far1_a, FAR_2)
    sib_cross_a, sib_cross_b = send(cross_a, FROM_HOME), send(cross_b, FROM_HOME)
    pick, masks = lax.optimization_barrier((pick, masks, near1_a))[:2]
    near3_a, back_a = send(near2_a, NEAR_3), send(jnp.where(s == 1, own, far2_a), BACK_3)
    near2_b, far2_b = send(jnp.where(s == 0, cross_b, near1_b), NEAR_2), send(far1_b, FAR_2)
    rows = prepare_rows(
        part,
        window_starts,
        lag_frames,
        plane,
        count,
        ((own, cross_a, sib_cross_b), (sib, cross_b, sib_cross_a)),
        window,
    )
    near2_b, far2_b, *rows = lax.optimization_barrier((near2_b, far2_b, *rows))
    near3_b, back_b = send(near2_b, NEAR_3), send(jnp.where(s == 1, sib, far2_b), BACK_3)

    outs = ()
    for where_to, pieces in (
        (part, (own, cross_a, near1_a, near2_a, near3_a, back_a, far2_a)),
        (1 - part, (sib, cross_b, near1_b, near2_b, near3_b, back_b, far2_b)),
    ):
        pieces = [piece.reshape(trajectories * half, features) for piece in pieces]
        outs = product(where_to, pick, count, masks, rows, pieces, outs)
    return outs


def solution(mesh):
    placed = (P("groups", "tm", ("feat", "sub")), P("groups"), P("groups"))
    line = mesh.shape["feat"] == 4 and mesh.shape["tm"] == 2 and mesh.shape["sub"] == 2
    return jax.shard_map(
        line_of_four if line else general,
        mesh=mesh,
        in_specs=placed,
        out_specs=(P(("groups", "feat"), ("tm", "sub")), P(("groups", "feat"), ("tm", "sub"))),
        check_vma=False,
    )
```

```python
import functools

import jax
import jax.numpy as jnp
from jax import lax
from jax.experimental import pallas as pl
from jax.experimental.pallas import tpu as pltpu
from jax.sharding import PartitionSpec as P

SLACK = 32
LAGMAX = 64
AXES = ("feat", "tm", "sub")
VMEM_LIMIT = 28 * 1024 * 1024
TILE = 512
DEPTH = 2
ROWS_TILE = 1024


def spread(x, axis, root):
    mine = lax.axis_index(axis) == root
    return lax.psum(jnp.where(mine, x, jnp.zeros_like(x)), axis)


def window_masks(window_starts, lag_frames, stored):
    instant = jnp.arange(stored, dtype=jnp.int32)[None, :]
    window_begin = window_starts[:, None]
    shift_by = lag_frames[:, None]
    finish = window_begin + (stored - SLACK)
    base_mask = (instant >= window_begin) & (instant < finish - shift_by)
    lag_mask = (instant >= window_begin + shift_by) & (instant < finish)
    return (base_mask.astype(jnp.bfloat16), lag_mask.astype(jnp.bfloat16))


def shift_ahead(series, lag_frames):
    stored = series.shape[1]
    padded = jnp.pad(series, ((0, 0), (0, LAGMAX), (0, 0)))

    def one_series(padded_rows, shift_by):
        return lax.dynamic_slice_in_dim(padded_rows, shift_by, stored, 0)

    return jax.vmap(one_series)(padded, lag_frames)


def frame_product(left, right):
    return lax.dot_general(
        left, right, (((0, 1), (0, 1)), ((), ())), preferred_element_type=jnp.float32
    )


def frame_mean(mask, series, frame_count):
    return jnp.einsum("kt,ktf->f", mask, series, preferred_element_type=jnp.float32) / frame_count


def general(frames, window_starts, lag_frames):
    halves = lax.all_gather(frames, "sub", axis=2, tiled=True)
    row_data = lax.all_gather(halves, "tm", axis=1, tiled=True)
    stored = row_data.shape[1]
    base_mask, lag_mask = window_masks(window_starts, lag_frames, stored)
    frame_count = (row_data.shape[0] * (stored - SLACK) - jnp.sum(lag_frames)).astype(jnp.float32)
    masked_rows = row_data * base_mask[:, :, None]
    row_mean = frame_mean(base_mask, row_data, frame_count)
    groups = lax.axis_size("tm") * lax.axis_size("sub")
    per_group = lax.axis_size("feat") // groups
    column = lax.axis_index("tm") * lax.axis_size("sub") + lax.axis_index("sub")
    tile_parts = []
    for member in range(per_group):
        column_block = spread(row_data, "feat", column * per_group + member)
        zero_mean = frame_mean(base_mask, column_block, frame_count)
        later_mean = frame_mean(lag_mask, column_block, frame_count)
        zero_part = (
            frame_product(masked_rows, column_block) / frame_count
            - row_mean[:, None] * zero_mean[None, :]
        )
        crossed = frame_product(masked_rows, shift_ahead(column_block, lag_frames))
        lag_part = crossed / frame_count - row_mean[:, None] * later_mean[None, :]
        tile_parts.append((zero_part, lag_part))
    covariance_zero = jnp.concatenate([entries[0] for entries in tile_parts], axis=1)
    covariance_lag = jnp.concatenate([entries[1] for entries in tile_parts], axis=1)
    return (covariance_zero, covariance_lag)


def rank(s, x, c):
    return ((3 - s if x else s) * 2 + x) * 2 + c


def home(s, x):
    return (3 - s if x else s) % 2


def hops(links):
    pairs = []
    for s, d, b in links:
        for x in range(2):
            to = rank(d, x, home(b, x)) if d >= 0 else rank(3 - s, 1 - x, home(b, x))
            pairs.append((rank(s, x, home(b, x)), to))
    return pairs


PLACES = [(s, x) for s in range(4) for x in range(2)]
CORES = [(rank(s, x, c), rank(s, x, 1 - c)) for s, x in PLACES for c in range(2)]
PLANES = [(rank(s, x, c), rank(3 - s, 1 - x, c)) for s, x in PLACES for c in range(2)]
NEAR_1 = hops([(0, 1, 0), (1, 2, 1), (2, 3, 2)])
FAR_1 = hops([(3, 2, 3), (2, 0, 2)])
NEAR_2 = hops([(0, 1, 0), (1, 2, 0), (2, 3, 1), (3, -1, 2)])
FAR_2 = hops([(2, 0, 3), (0, -1, 2)])
NEAR_3 = hops([(1, 2, 0), (2, 3, 0)])
BACK_3 = hops([(3, 2, 1), (0, -1, 3)])
OWN_3 = hops([(1, 0, 1)])
PICKS = (((0, 2, 3, 4), (1, 3, 4, 5)), ((7, 0, 2, 3), (3, 1, 5, 6)))


def send(x, pairs):
    return lax.ppermute(x, AXES, pairs)


def after(value, *others):
    return lax.optimization_barrier((value, *others))[0]


def dot(left, right):
    return jnp.dot(left, right, preferred_element_type=jnp.float32)


def rows_kernel(
    starts_ref, lags_ref, x_ref, count_ref, parts, zero_ref, late_ref, mean_ref, moves_ref, *, window
):
    trajectories, half = parts[0][0].shape[0], parts[0][0].shape[1]
    stored = 2 * half
    p, i = pl.program_id(0), pl.program_id(1)

    @pl.when((p == 0) & (i == 0))
    def _():
        def instant(axis):
            n = lax.broadcasted_iota(jnp.int32, (stored, stored), axis)
            return jnp.where(x_ref[0] == 0, n, lax.rem(n + half, stored))

        frame, column = instant(0), instant(1)
        for k in range(trajectories):
            start, lag = starts_ref[k], lags_ref[k]
            kept = (frame >= start) & (frame < start + window - lag)
            for n, ahead in enumerate((0, lag)):
                moves_ref[k, :, n * stored : (n + 1) * stored] = jnp.where(
                    kept & (column == frame + ahead), 1.0, 0.0
                ).astype(jnp.bfloat16)

    def fill(own_ref, cross_ref):
        total = None
        for k in range(trajectories):
            series = jnp.concatenate([own_ref[k], cross_ref[k]], axis=0)
            moved = lax.dot_general(
                series,
                moves_ref[k],
                (((0,), (0,)), ((), ())),
                preferred_element_type=jnp.float32,
            )
            total = moved[:, :stored] if total is None else total + moved[:, :stored]
            moved = moved.astype(jnp.bfloat16)
            for n, ref in enumerate((zero_ref, late_ref)):
                for side in range(2):
                    to, at = (side * trajectories + k) * half, n * stored + side * half
                    ref[:, to : to + half] = moved[:, at : at + half]
        mean = jnp.sum(total, axis=1, keepdims=True) / count_ref[0]
        mean_ref[...] = jnp.broadcast_to(mean, mean_ref.shape)

    for n, (own_ref, cross_ref) in enumerate(parts):
        pl.when(p == n)(functools.partial(fill, own_ref, cross_ref))


def prepare_rows(part, starts, lags, x, count, arrays, window):
    trajectories, half, features = arrays[0][0].shape
    tile = min(ROWS_TILE, features)
    steps = features // tile
    depth = trajectories * 2 * half
    row = jax.ShapeDtypeStruct((2 * features, depth), jnp.bfloat16)
    mean = jax.ShapeDtypeStruct((2 * features, 128), jnp.float32)

    def spot(p, i, part_ref, *_):
        return (jnp.where(p == 0, part_ref[0], 1 - part_ref[0]) * steps + i, 0)

    shape = (trajectories, half, tile)
    first = pl.BlockSpec(shape, lambda p, i, *_: (0, 0, jnp.where(p == 0, i, steps - 1)))
    second = pl.BlockSpec(shape, lambda p, i, *_: (0, 0, jnp.where(p == 0, 0, i)))

    def body(part_ref, starts_ref, lags_ref, x_ref, count_ref, *refs):
        rows_kernel(
            starts_ref, lags_ref, x_ref, count_ref, (refs[:2], refs[2:4]), *refs[4:], window=window
        )

    return pl.pallas_call(
        body,
        out_shape=(row, row, mean),
        grid_spec=pltpu.PrefetchScalarGridSpec(
            num_scalar_prefetch=5,
            grid=(2, steps),
            in_specs=[first] * 2 + [second] * 2,
            out_specs=[
                pl.BlockSpec((tile, depth), spot),
                pl.BlockSpec((tile, depth), spot),
                pl.BlockSpec((tile, 128), spot),
            ],
            scratch_shapes=[pltpu.VMEM((trajectories, 2 * half, 4 * half), jnp.bfloat16)],
        ),
        compiler_params=pltpu.CompilerParams(vmem_limit_bytes=VMEM_LIMIT),
        cost_estimate=pl.CostEstimate(
            flops=0, bytes_accessed=28 * arrays[0][0].size, transcendentals=0
        ),
        name="rows",
    )(part, starts, lags, x, count, *arrays[0], *arrays[1])


def product_kernel(part_ref, place_ref, count_ref, masks_ref, mean_ref, zero_ref, late_ref, *refs, n_pieces):
    pieces = refs[:n_pieces]
    cov_zero_ref, cov_late_ref, left_ref, columns_ref, made_ref, arrived, fetched, stored = refs[-8:]
    half, width = columns_ref.shape[0] // 2, columns_ref.shape[1]
    tile = left_ref.shape[2]
    steps = left_ref.shape[1]
    depth_out = made_ref.shape[0]
    scale = 1.0 / count_ref[0]
    first = pl.multiple_of(part_ref[0] * width, width)

    def piece_copy(piece, side):
        return pltpu.make_async_copy(
            piece, columns_ref.at[pl.ds(side * half, half)], arrived.at[side]
        )

    def left_copy(n, i):
        return pltpu.make_async_copy(
            (zero_ref, late_ref)[n].at[pl.ds(i * tile, tile)], left_ref.at[n, i], fetched.at[n, i]
        )

    def out_copy(n, i):
        slot = lax.rem(i, depth_out)
        return pltpu.make_async_copy(
            made_ref.at[slot, n],
            (cov_zero_ref, cov_late_ref)[n].at[pl.ds(i * tile, tile), pl.ds(first, width)],
            stored.at[slot, n],
        )

    for kind, sides in enumerate(PICKS):
        for side, places in enumerate(sides):
            for place, m in enumerate(places):

                @pl.when((place_ref[0] == place) & (place_ref[1] == kind))
                def _():
                    piece_copy(pieces[m], side).start()

    def fetch(i):
        for n in range(2):
            left_copy(n, i).start()

    fetch(0)
    for side in range(2):
        piece_copy(pieces[0], side).wait()
    means = dot(masks_ref[...], columns_ref[...]) * scale

    def step(i, carry):
        @pl.when(i + 1 < steps)
        def _():
            fetch(i + 1)

        row_mean = mean_ref[pl.ds(pl.multiple_of(i * tile, tile), tile), :1]
        for n in range(2):
            left_copy(n, i).wait()

            @pl.when(i >= depth_out)
            def _():
                out_copy(n, i - depth_out).wait()

            total = dot(left_ref[n, i], columns_ref[...])
            made_ref[lax.rem(i, depth_out), n] = total * scale - row_mean * means[8 * n : 8 * n + 1]
            out_copy(n, i).start()
        return carry

    lax.fori_loop(0, steps, step, 0)
    for i in range(max(0, steps - depth_out), steps):
        for n in range(2):
            out_copy(n, i).wait()


def product(part, place, count, masks, rows, pieces, before):
    zero, late, means = rows
    height, depth = zero.shape
    width = pieces[0].shape[-1]
    tile = min(TILE, height)
    steps = height // tile
    out = jax.ShapeDtypeStruct((height, 2 * width), jnp.float32)
    anywhere = pl.BlockSpec(memory_space=pl.ANY)
    return pl.pallas_call(
        functools.partial(product_kernel, n_pieces=len(pieces)),
        out_shape=(out, out),
        grid_spec=pltpu.PrefetchScalarGridSpec(
            num_scalar_prefetch=3,
            grid=(1,),
            in_specs=[
                pl.BlockSpec((16, depth), lambda i, *_: (0, 0)),
                pl.BlockSpec((height, 128), lambda i, *_: (0, 0)),
            ]
            + [anywhere] * (2 + len(pieces) + len(before)),
            out_specs=[anywhere] * 2,
            scratch_shapes=[
                pltpu.VMEM((2, steps, tile, depth), jnp.bfloat16),
                pltpu.VMEM((depth, width), jnp.bfloat16),
                pltpu.VMEM((DEPTH, 2, tile, width), jnp.float32),
                pltpu.SemaphoreType.DMA((2,)),
                pltpu.SemaphoreType.DMA((2, steps)),
                pltpu.SemaphoreType.DMA((DEPTH, 2)),
            ],
        ),
        input_output_aliases={7 + len(pieces) + i: i for i in range(len(before))},
        compiler_params=pltpu.CompilerParams(vmem_limit_bytes=VMEM_LIMIT),
        cost_estimate=pl.CostEstimate(
            flops=4 * height * depth * width,
            bytes_accessed=4 * height * depth + 8 * height * width,
            transcendentals=0,
        ),
        name="covariances",
    )(part, place, count, masks, means, zero, late, *pieces, *before)


def line_of_four(frames, window_starts, lag_frames):
    trajectories, half, features = frames.shape
    stored = 2 * half
    window = stored - SLACK
    z, x, c = (lax.axis_index(a) for a in AXES)
    s = jnp.where(x == 1, 3 - z, z)
    count = (trajectories * window - jnp.sum(lag_frames)).astype(jnp.float32).reshape(1)
    plane = x.astype(jnp.int32).reshape(1)
    part = c.astype(jnp.int32).reshape(1)

    base_mask, lag_mask = window_masks(window_starts, lag_frames, stored)

    def relative(mask):
        low, high = mask[:, :half].reshape(-1), mask[:, half:].reshape(-1)
        return jnp.where(x == 0, jnp.concatenate([low, high]), jnp.concatenate([high, low]))

    masks = jnp.concatenate(
        [
            jnp.broadcast_to(relative(m)[None, :], (8, trajectories * stored))
            for m in (base_mask, lag_mask)
        ]
    )

    picks = jnp.array([[[0, 2, 3, 4], [1, 3, 4, 5]], [[5, 0, 2, 3], [3, 1, 5, 6]]], jnp.int32)
    pick = picks[jnp.where(c == x, 0, 1), :, s]

    place = jnp.stack([s, jnp.where(c == x, 0, 1)]).astype(jnp.int32)
    own = frames
    near1_a, far1_a = send(own, NEAR_1), send(own, FAR_1)
    cross = send(own, PLANES)
    sib = send(own, CORES)
    near1_b, far1_b = send(sib, NEAR_1), send(sib, FAR_1)
    near1_a, far1_a, masks, count, place = lax.optimization_barrier(
        (near1_a, far1_a, masks, count, place)
    )
    near2_a, far2_a = send(jnp.where(s == 0, cross, near1_a), NEAR_2), send(far1_a, FAR_2)
    sib_cross = send(cross, CORES)
    near2_b, far2_b = send(jnp.where(s == 0, sib_cross, near1_b), NEAR_2), send(far1_b, FAR_2)
    near3_a, back_a, close_a = send(near2_a, NEAR_3), send(far2_a, BACK_3), send(own, OWN_3)
    rows = prepare_rows(
        part, window_starts, lag_frames, plane, count, ((own, cross), (sib, sib_cross)), window
    )
    near2_b, far2_b, *rows = lax.optimization_barrier((near2_b, far2_b, *rows))
    near3_b, back_b, close_b = send(near2_b, NEAR_3), send(far2_b, BACK_3), send(sib, OWN_3)

    outs = ()
    for where_to, pieces in (
        (part, (own, cross, near1_a, near2_a, near3_a, back_a, far2_a, close_a)),
        (1 - part, (sib, sib_cross, near1_b, near2_b, near3_b, back_b, far2_b, close_b)),
    ):
        pieces = [piece.reshape(trajectories * half, features) for piece in pieces]
        outs = product(where_to, place, count, masks, rows, pieces, outs)
    return outs


def solution(mesh):
    placed = (P("groups", "tm", ("feat", "sub")), P("groups"), P("groups"))
    line = mesh.shape["feat"] == 4 and mesh.shape["tm"] == 2 and mesh.shape["sub"] == 2
    return jax.shard_map(
        line_of_four if line else general,
        mesh=mesh,
        in_specs=placed,
        out_specs=(P(("groups", "feat"), ("tm", "sub")), P(("groups", "feat"), ("tm", "sub"))),
        check_vma=False,
    )
```

```python
import functools

import jax
import jax.numpy as jnp
from jax import lax
from jax.experimental import pallas as pl
from jax.experimental.pallas import tpu as pltpu
from jax.sharding import PartitionSpec as P

SLACK = 32
LAGMAX = 64
AXES = ("feat", "tm", "sub")
VMEM_LIMIT = 32 * 1024 * 1024
TILES = (1024, 768, 256)
DEPTH = 2
ROWS_TILE = 1024


def spread(x, axis, root):
    mine = lax.axis_index(axis) == root
    return lax.psum(jnp.where(mine, x, jnp.zeros_like(x)), axis)


def window_masks(window_starts, lag_frames, stored):
    instant = jnp.arange(stored, dtype=jnp.int32)[None, :]
    window_begin = window_starts[:, None]
    shift_by = lag_frames[:, None]
    finish = window_begin + (stored - SLACK)
    base_mask = (instant >= window_begin) & (instant < finish - shift_by)
    lag_mask = (instant >= window_begin + shift_by) & (instant < finish)
    return (base_mask.astype(jnp.bfloat16), lag_mask.astype(jnp.bfloat16))


def shift_ahead(series, lag_frames):
    stored = series.shape[1]
    padded = jnp.pad(series, ((0, 0), (0, LAGMAX), (0, 0)))

    def one_series(padded_rows, shift_by):
        return lax.dynamic_slice_in_dim(padded_rows, shift_by, stored, 0)

    return jax.vmap(one_series)(padded, lag_frames)


def frame_product(left, right):
    return lax.dot_general(
        left, right, (((0, 1), (0, 1)), ((), ())), preferred_element_type=jnp.float32
    )


def frame_mean(mask, series, frame_count):
    return jnp.einsum("kt,ktf->f", mask, series, preferred_element_type=jnp.float32) / frame_count


def general(frames, window_starts, lag_frames):
    halves = lax.all_gather(frames, "sub", axis=2, tiled=True)
    row_data = lax.all_gather(halves, "tm", axis=1, tiled=True)
    stored = row_data.shape[1]
    base_mask, lag_mask = window_masks(window_starts, lag_frames, stored)
    frame_count = (row_data.shape[0] * (stored - SLACK) - jnp.sum(lag_frames)).astype(jnp.float32)
    masked_rows = row_data * base_mask[:, :, None]
    row_mean = frame_mean(base_mask, row_data, frame_count)
    groups = lax.axis_size("tm") * lax.axis_size("sub")
    per_group = lax.axis_size("feat") // groups
    column = lax.axis_index("tm") * lax.axis_size("sub") + lax.axis_index("sub")
    tile_parts = []
    for member in range(per_group):
        column_block = spread(row_data, "feat", column * per_group + member)
        zero_mean = frame_mean(base_mask, column_block, frame_count)
        later_mean = frame_mean(lag_mask, column_block, frame_count)
        zero_part = (
            frame_product(masked_rows, column_block) / frame_count
            - row_mean[:, None] * zero_mean[None, :]
        )
        crossed = frame_product(masked_rows, shift_ahead(column_block, lag_frames))
        lag_part = crossed / frame_count - row_mean[:, None] * later_mean[None, :]
        tile_parts.append((zero_part, lag_part))
    covariance_zero = jnp.concatenate([entries[0] for entries in tile_parts], axis=1)
    covariance_lag = jnp.concatenate([entries[1] for entries in tile_parts], axis=1)
    return (covariance_zero, covariance_lag)


def rank(s, x, c):
    return ((3 - s if x else s) * 2 + x) * 2 + c


def home(s, x):
    return (3 - s if x else s) % 2


def hops(links):
    pairs = []
    for s, d, b in links:
        for x in range(2):
            to = rank(d, x, home(b, x)) if d >= 0 else rank(3 - s, 1 - x, home(b, x))
            pairs.append((rank(s, x, home(b, x)), to))
    return pairs


PLACES = [(s, x) for s in range(4) for x in range(2)]
CORES = [(rank(s, x, c), rank(s, x, 1 - c)) for s, x in PLACES for c in range(2)]
PLANES = [(rank(s, x, c), rank(3 - s, 1 - x, c)) for s, x in PLACES for c in range(2)]
NEAR_1 = hops([(0, 1, 0), (1, 2, 1), (2, 3, 2)])
FAR_1 = hops([(3, 2, 3), (2, 0, 2)])
NEAR_2 = hops([(0, 1, 0), (1, 2, 0), (2, 3, 1), (3, -1, 2)])
FAR_2 = hops([(2, 0, 3), (0, -1, 2)])
NEAR_3 = hops([(1, 2, 0), (2, 3, 0)])
BACK_3 = hops([(3, 2, 1), (0, -1, 3)])
OWN_3 = hops([(1, 0, 1)])
PICKS = (((0, 2, 3, 4), (1, 3, 4, 5)), ((7, 0, 2, 3), (3, 1, 5, 6)))


def send(x, pairs):
    return lax.ppermute(x, AXES, pairs)


def after(value, *others):
    return lax.optimization_barrier((value, *others))[0]


def dot(left, right):
    return jnp.dot(left, right, preferred_element_type=jnp.float32)


def rows_kernel(
    starts_ref, lags_ref, x_ref, count_ref, parts, zero_ref, late_ref, mean_ref, moves_ref, *, window
):
    trajectories, half = parts[0][0].shape[0], parts[0][0].shape[1]
    stored = 2 * half
    p, i = pl.program_id(0), pl.program_id(1)

    @pl.when((p == 0) & (i == 0))
    def _():
        def instant(axis):
            n = lax.broadcasted_iota(jnp.int32, (stored, stored), axis)
            return jnp.where(x_ref[0] == 0, n, lax.rem(n + half, stored))

        frame, column = instant(0), instant(1)
        for k in range(trajectories):
            start, lag = starts_ref[k], lags_ref[k]
            kept = (frame >= start) & (frame < start + window - lag)
            for n, ahead in enumerate((0, lag)):
                moves_ref[k, :, n * stored : (n + 1) * stored] = jnp.where(
                    kept & (column == frame + ahead), 1.0, 0.0
                ).astype(jnp.bfloat16)

    def fill(own_ref, cross_ref):
        total = None
        for k in range(trajectories):
            series = jnp.concatenate([own_ref[k], cross_ref[k]], axis=0)
            moved = lax.dot_general(
                series,
                moves_ref[k],
                (((0,), (0,)), ((), ())),
                preferred_element_type=jnp.float32,
            )
            total = moved[:, :stored] if total is None else total + moved[:, :stored]
            moved = moved.astype(jnp.bfloat16)
            for n, ref in enumerate((zero_ref, late_ref)):
                for side in range(2):
                    to, at = (side * trajectories + k) * half, n * stored + side * half
                    ref[:, to : to + half] = moved[:, at : at + half]
        mean = jnp.sum(total, axis=1, keepdims=True) / count_ref[0]
        mean_ref[...] = jnp.broadcast_to(mean, mean_ref.shape)

    for n, (own_ref, cross_ref) in enumerate(parts):
        pl.when(p == n)(functools.partial(fill, own_ref, cross_ref))


def prepare_rows(part, starts, lags, x, count, arrays, window):
    trajectories, half, features = arrays[0][0].shape
    tile = min(ROWS_TILE, features)
    steps = features // tile
    depth = trajectories * 2 * half
    row = jax.ShapeDtypeStruct((2 * features, depth), jnp.bfloat16)
    mean = jax.ShapeDtypeStruct((2 * features, 128), jnp.float32)

    def spot(p, i, part_ref, *_):
        return (jnp.where(p == 0, part_ref[0], 1 - part_ref[0]) * steps + i, 0)

    shape = (trajectories, half, tile)
    first = pl.BlockSpec(shape, lambda p, i, *_: (0, 0, jnp.where(p == 0, i, steps - 1)))
    second = pl.BlockSpec(shape, lambda p, i, *_: (0, 0, jnp.where(p == 0, 0, i)))

    def body(part_ref, starts_ref, lags_ref, x_ref, count_ref, *refs):
        rows_kernel(
            starts_ref, lags_ref, x_ref, count_ref, (refs[:2], refs[2:4]), *refs[4:], window=window
        )

    return pl.pallas_call(
        body,
        out_shape=(row, row, mean),
        grid_spec=pltpu.PrefetchScalarGridSpec(
            num_scalar_prefetch=5,
            grid=(2, steps),
            in_specs=[first] * 2 + [second] * 2,
            out_specs=[
                pl.BlockSpec((tile, depth), spot),
                pl.BlockSpec((tile, depth), spot),
                pl.BlockSpec((tile, 128), spot),
            ],
            scratch_shapes=[pltpu.VMEM((trajectories, 2 * half, 4 * half), jnp.bfloat16)],
        ),
        compiler_params=pltpu.CompilerParams(vmem_limit_bytes=VMEM_LIMIT),
        cost_estimate=pl.CostEstimate(
            flops=0, bytes_accessed=28 * arrays[0][0].size, transcendentals=0
        ),
        name="rows",
    )(part, starts, lags, x, count, *arrays[0], *arrays[1])


def product_kernel(part_ref, place_ref, count_ref, masks_ref, mean_ref, zero_ref, late_ref, *refs, n_pieces, tiles):
    pieces = refs[:n_pieces]
    cov_zero_ref, cov_late_ref, left_ref, columns_ref, made_ref, arrived, fetched, stored = refs[-8:]
    half, width = columns_ref.shape[0] // 2, columns_ref.shape[1]
    scale = 1.0 / count_ref[0]
    first = pl.multiple_of(part_ref[0] * width, width)

    def piece_copy(piece, side):
        return pltpu.make_async_copy(
            piece, columns_ref.at[pl.ds(side * half, half)], arrived.at[side]
        )

    def left_copy(n, i):
        rows = pl.ds(*tiles[i])
        return pltpu.make_async_copy(
            (zero_ref, late_ref)[n].at[rows], left_ref.at[n, rows], fetched.at[n, i]
        )

    def out_copy(n, i):
        slot = i % DEPTH
        return pltpu.make_async_copy(
            made_ref.at[slot, n, pl.ds(0, tiles[i][1])],
            (cov_zero_ref, cov_late_ref)[n].at[pl.ds(*tiles[i]), pl.ds(first, width)],
            stored.at[slot, n],
        )

    for kind, sides in enumerate(PICKS):
        for side, places in enumerate(sides):
            for place, m in enumerate(places):

                @pl.when((place_ref[0] == place) & (place_ref[1] == kind))
                def _():
                    piece_copy(pieces[m], side).start()

    for n in range(2):
        left_copy(n, 0).start()
    for side in range(2):
        piece_copy(pieces[0], side).wait()
    for i, (top, tile) in enumerate(tiles):
        if i + 1 < len(tiles):
            for n in range(2):
                left_copy(n, i + 1).start()
        if i == 0:
            means = dot(masks_ref[...], columns_ref[...]) * scale
        row_mean = mean_ref[top : top + tile, :1]
        for n in range(2):
            left_copy(n, i).wait()
            if i >= DEPTH:
                out_copy(n, i - DEPTH).wait()
            total = dot(left_ref[n, top : top + tile], columns_ref[...])
            made_ref[i % DEPTH, n, :tile] = total * scale - row_mean * means[8 * n : 8 * n + 1]
            out_copy(n, i).start()
    for i in range(max(0, len(tiles) - DEPTH), len(tiles)):
        for n in range(2):
            out_copy(n, i).wait()


def product(part, place, count, masks, rows, pieces, before):
    zero, late, means = rows
    height, depth = zero.shape
    width = pieces[0].shape[-1]
    tiles, top = [], 0
    for tile in TILES:
        tile = min(tile, height - top)
        tiles.append((top, tile))
        top += tile
    steps, tile = len(tiles), max(TILES)
    out = jax.ShapeDtypeStruct((height, 2 * width), jnp.float32)
    anywhere = pl.BlockSpec(memory_space=pl.ANY)
    return pl.pallas_call(
        functools.partial(product_kernel, n_pieces=len(pieces), tiles=tiles),
        out_shape=(out, out),
        grid_spec=pltpu.PrefetchScalarGridSpec(
            num_scalar_prefetch=3,
            grid=(1,),
            in_specs=[
                pl.BlockSpec((16, depth), lambda i, *_: (0, 0)),
                pl.BlockSpec((height, 128), lambda i, *_: (0, 0)),
            ]
            + [anywhere] * (2 + len(pieces) + len(before)),
            out_specs=[anywhere] * 2,
            scratch_shapes=[
                pltpu.VMEM((2, height, depth), jnp.bfloat16),
                pltpu.VMEM((depth, width), jnp.bfloat16),
                pltpu.VMEM((DEPTH, 2, tile, width), jnp.float32),
                pltpu.SemaphoreType.DMA((2,)),
                pltpu.SemaphoreType.DMA((2, steps)),
                pltpu.SemaphoreType.DMA((DEPTH, 2)),
            ],
        ),
        input_output_aliases={7 + len(pieces) + i: i for i in range(len(before))},
        compiler_params=pltpu.CompilerParams(vmem_limit_bytes=VMEM_LIMIT),
        cost_estimate=pl.CostEstimate(
            flops=4 * height * depth * width,
            bytes_accessed=4 * height * depth + 8 * height * width,
            transcendentals=0,
        ),
        name="covariances",
    )(part, place, count, masks, means, zero, late, *pieces, *before)


def line_of_four(frames, window_starts, lag_frames):
    trajectories, half, features = frames.shape
    stored = 2 * half
    window = stored - SLACK
    z, x, c = (lax.axis_index(a) for a in AXES)
    s = jnp.where(x == 1, 3 - z, z)
    count = (trajectories * window - jnp.sum(lag_frames)).astype(jnp.float32).reshape(1)
    plane = x.astype(jnp.int32).reshape(1)
    part = c.astype(jnp.int32).reshape(1)

    base_mask, lag_mask = window_masks(window_starts, lag_frames, stored)

    def relative(mask):
        low, high = mask[:, :half].reshape(-1), mask[:, half:].reshape(-1)
        return jnp.where(x == 0, jnp.concatenate([low, high]), jnp.concatenate([high, low]))

    masks = jnp.concatenate(
        [
            jnp.broadcast_to(relative(m)[None, :], (8, trajectories * stored))
            for m in (base_mask, lag_mask)
        ]
    )

    picks = jnp.array([[[0, 2, 3, 4], [1, 3, 4, 5]], [[5, 0, 2, 3], [3, 1, 5, 6]]], jnp.int32)
    pick = picks[jnp.where(c == x, 0, 1), :, s]

    place = jnp.stack([s, jnp.where(c == x, 0, 1)]).astype(jnp.int32)
    own = frames
    near1_a, far1_a = send(own, NEAR_1), send(own, FAR_1)
    cross = send(own, PLANES)
    sib = send(own, CORES)
    near1_b, far1_b = send(sib, NEAR_1), send(sib, FAR_1)
    near1_a, far1_a, masks, count, place = lax.optimization_barrier(
        (near1_a, far1_a, masks, count, place)
    )
    near2_a, far2_a = send(jnp.where(s == 0, cross, near1_a), NEAR_2), send(far1_a, FAR_2)
    sib_cross = send(cross, CORES)
    near2_b, far2_b = send(jnp.where(s == 0, sib_cross, near1_b), NEAR_2), send(far1_b, FAR_2)
    near3_a, back_a, close_a = send(near2_a, NEAR_3), send(far2_a, BACK_3), send(after(own, near2_a, far2_a), OWN_3)
    rows = prepare_rows(
        part, window_starts, lag_frames, plane, count, ((own, cross), (sib, sib_cross)), window
    )
    near2_b, far2_b, *rows = lax.optimization_barrier((near2_b, far2_b, *rows))
    near3_b, back_b, close_b = send(near2_b, NEAR_3), send(far2_b, BACK_3), send(after(sib, near2_b), OWN_3)

    outs = ()
    for where_to, pieces in (
        (part, (own, cross, near1_a, near2_a, near3_a, back_a, far2_a, close_a)),
        (1 - part, (sib, sib_cross, near1_b, near2_b, near3_b, back_b, far2_b, close_b)),
    ):
        pieces = [piece.reshape(trajectories * half, features) for piece in pieces]
        outs = product(where_to, place, count, masks, rows, pieces, outs)
    return outs


def solution(mesh):
    placed = (P("groups", "tm", ("feat", "sub")), P("groups"), P("groups"))
    line = mesh.shape["feat"] == 4 and mesh.shape["tm"] == 2 and mesh.shape["sub"] == 2
    return jax.shard_map(
        line_of_four if line else general,
        mesh=mesh,
        in_specs=placed,
        out_specs=(P(("groups", "feat"), ("tm", "sub")), P(("groups", "feat"), ("tm", "sub"))),
        check_vma=False,
    )
```

```python
import functools

import jax
import jax.numpy as jnp
from jax import lax
from jax.experimental import pallas as pl
from jax.experimental.pallas import tpu as pltpu
from jax.sharding import PartitionSpec as P

SLACK = 32
LAGMAX = 64
AXES = ("feat", "tm", "sub")
VMEM_LIMIT = 32 * 1024 * 1024
TILES = (1024, 768, 256)
DEPTH = 2
ROWS_TILE = 1024


def spread(x, axis, root):
    mine = lax.axis_index(axis) == root
    return lax.psum(jnp.where(mine, x, jnp.zeros_like(x)), axis)


def window_masks(window_starts, lag_frames, stored):
    instant = jnp.arange(stored, dtype=jnp.int32)[None, :]
    window_begin = window_starts[:, None]
    shift_by = lag_frames[:, None]
    finish = window_begin + (stored - SLACK)
    base_mask = (instant >= window_begin) & (instant < finish - shift_by)
    lag_mask = (instant >= window_begin + shift_by) & (instant < finish)
    return (base_mask.astype(jnp.bfloat16), lag_mask.astype(jnp.bfloat16))


def shift_ahead(series, lag_frames):
    stored = series.shape[1]
    padded = jnp.pad(series, ((0, 0), (0, LAGMAX), (0, 0)))

    def one_series(padded_rows, shift_by):
        return lax.dynamic_slice_in_dim(padded_rows, shift_by, stored, 0)

    return jax.vmap(one_series)(padded, lag_frames)


def frame_product(left, right):
    return lax.dot_general(
        left, right, (((0, 1), (0, 1)), ((), ())), preferred_element_type=jnp.float32
    )


def frame_mean(mask, series, frame_count):
    return jnp.einsum("kt,ktf->f", mask, series, preferred_element_type=jnp.float32) / frame_count


def general(frames, window_starts, lag_frames):
    halves = lax.all_gather(frames, "sub", axis=2, tiled=True)
    row_data = lax.all_gather(halves, "tm", axis=1, tiled=True)
    stored = row_data.shape[1]
    base_mask, lag_mask = window_masks(window_starts, lag_frames, stored)
    frame_count = (row_data.shape[0] * (stored - SLACK) - jnp.sum(lag_frames)).astype(jnp.float32)
    masked_rows = row_data * base_mask[:, :, None]
    row_mean = frame_mean(base_mask, row_data, frame_count)
    groups = lax.axis_size("tm") * lax.axis_size("sub")
    per_group = lax.axis_size("feat") // groups
    column = lax.axis_index("tm") * lax.axis_size("sub") + lax.axis_index("sub")
    tile_parts = []
    for member in range(per_group):
        column_block = spread(row_data, "feat", column * per_group + member)
        zero_mean = frame_mean(base_mask, column_block, frame_count)
        later_mean = frame_mean(lag_mask, column_block, frame_count)
        zero_part = (
            frame_product(masked_rows, column_block) / frame_count
            - row_mean[:, None] * zero_mean[None, :]
        )
        crossed = frame_product(masked_rows, shift_ahead(column_block, lag_frames))
        lag_part = crossed / frame_count - row_mean[:, None] * later_mean[None, :]
        tile_parts.append((zero_part, lag_part))
    covariance_zero = jnp.concatenate([entries[0] for entries in tile_parts], axis=1)
    covariance_lag = jnp.concatenate([entries[1] for entries in tile_parts], axis=1)
    return (covariance_zero, covariance_lag)


def rank(s, x, c):
    return ((3 - s if x else s) * 2 + x) * 2 + c


def home(s, x):
    return (3 - s if x else s) % 2


def hops(links):
    pairs = []
    for s, d, b in links:
        for x in range(2):
            to = rank(d, x, home(b, x)) if d >= 0 else rank(3 - s, 1 - x, home(b, x))
            pairs.append((rank(s, x, home(b, x)), to))
    return pairs


PLACES = [(s, x) for s in range(4) for x in range(2)]
CORES = [(rank(s, x, c), rank(s, x, 1 - c)) for s, x in PLACES for c in range(2)]
PLANES = [(rank(s, x, c), rank(3 - s, 1 - x, c)) for s, x in PLACES for c in range(2)]
NEAR_1 = hops([(0, 1, 0), (1, 2, 1), (2, 3, 2)])
FAR_1 = hops([(3, 2, 3), (2, 0, 2)])
NEAR_2 = hops([(0, 1, 0), (1, 2, 0), (2, 3, 1), (3, -1, 2)])
FAR_2 = hops([(2, 0, 3), (0, -1, 2)])
NEAR_3 = hops([(1, 2, 0), (2, 3, 0)])
BACK_3 = hops([(3, 2, 1), (0, -1, 3)])
OWN_3 = hops([(1, 0, 1)])
PICKS = (((0, 2, 3, 4), (1, 3, 4, 5)), ((7, 0, 2, 3), (3, 1, 5, 6)))


def send(x, pairs):
    return lax.ppermute(x, AXES, pairs)


def after(value, *others):
    return lax.optimization_barrier((value, *others))[0]


def dot(left, right):
    return jnp.dot(left, right, preferred_element_type=jnp.float32)


def rows_kernel(
    starts_ref, lags_ref, x_ref, count_ref, parts, zero_ref, late_ref, mean_ref, moves_ref, *, window
):
    trajectories, half = parts[0][0].shape[0], parts[0][0].shape[1]
    stored = 2 * half
    p, i = pl.program_id(0), pl.program_id(1)

    @pl.when((p == 0) & (i == 0))
    def _():
        def instant(axis):
            n = lax.broadcasted_iota(jnp.int32, (stored, stored), axis)
            return jnp.where(x_ref[0] == 0, n, lax.rem(n + half, stored))

        frame, column = instant(0), instant(1)
        for k in range(trajectories):
            start, lag = starts_ref[k], lags_ref[k]
            kept = (frame >= start) & (frame < start + window - lag)
            for n, ahead in enumerate((0, lag)):
                moves_ref[k, :, n * stored : (n + 1) * stored] = jnp.where(
                    kept & (column == frame + ahead), 1.0, 0.0
                ).astype(jnp.bfloat16)

    def fill(own_ref, cross_ref):
        total = None
        for k in range(trajectories):
            series = jnp.concatenate([own_ref[k], cross_ref[k]], axis=0)
            moved = lax.dot_general(
                series,
                moves_ref[k],
                (((0,), (0,)), ((), ())),
                preferred_element_type=jnp.float32,
            )
            total = moved[:, :stored] if total is None else total + moved[:, :stored]
            moved = moved.astype(jnp.bfloat16)
            for n, ref in enumerate((zero_ref, late_ref)):
                for side in range(2):
                    to, at = (side * trajectories + k) * half, n * stored + side * half
                    ref[:, to : to + half] = moved[:, at : at + half]
        mean = jnp.sum(total, axis=1, keepdims=True) / count_ref[0]
        mean_ref[...] = jnp.broadcast_to(mean, mean_ref.shape)

    for n, (own_ref, cross_ref) in enumerate(parts):
        pl.when(p == n)(functools.partial(fill, own_ref, cross_ref))


def prepare_rows(part, starts, lags, x, count, arrays, window):
    trajectories, half, features = arrays[0][0].shape
    tile = min(ROWS_TILE, features)
    steps = features // tile
    depth = trajectories * 2 * half
    row = jax.ShapeDtypeStruct((2 * features, depth), jnp.bfloat16)
    mean = jax.ShapeDtypeStruct((2 * features, 128), jnp.float32)

    def spot(p, i, part_ref, *_):
        return (jnp.where(p == 0, part_ref[0], 1 - part_ref[0]) * steps + i, 0)

    shape = (trajectories, half, tile)
    first = pl.BlockSpec(shape, lambda p, i, *_: (0, 0, jnp.where(p == 0, i, steps - 1)))
    second = pl.BlockSpec(shape, lambda p, i, *_: (0, 0, jnp.where(p == 0, 0, i)))

    def body(part_ref, starts_ref, lags_ref, x_ref, count_ref, *refs):
        rows_kernel(
            starts_ref, lags_ref, x_ref, count_ref, (refs[:2], refs[2:4]), *refs[4:], window=window
        )

    return pl.pallas_call(
        body,
        out_shape=(row, row, mean),
        grid_spec=pltpu.PrefetchScalarGridSpec(
            num_scalar_prefetch=5,
            grid=(2, steps),
            in_specs=[first] * 2 + [second] * 2,
            out_specs=[
                pl.BlockSpec((tile, depth), spot),
                pl.BlockSpec((tile, depth), spot),
                pl.BlockSpec((tile, 128), spot),
            ],
            scratch_shapes=[pltpu.VMEM((trajectories, 2 * half, 4 * half), jnp.bfloat16)],
        ),
        compiler_params=pltpu.CompilerParams(vmem_limit_bytes=VMEM_LIMIT),
        cost_estimate=pl.CostEstimate(
            flops=0, bytes_accessed=28 * arrays[0][0].size, transcendentals=0
        ),
        name="rows",
    )(part, starts, lags, x, count, *arrays[0], *arrays[1])


def product_kernel(part_ref, place_ref, count_ref, masks_ref, mean_ref, zero_ref, late_ref, *refs, n_pieces, tiles):
    pieces = refs[:n_pieces]
    cov_zero_ref, cov_late_ref, columns_ref, made_ref, arrived, stored = refs[-6:]
    half, width = columns_ref.shape[0] // 2, columns_ref.shape[1]
    scale = 1.0 / count_ref[0]
    first = pl.multiple_of(part_ref[0] * width, width)

    def piece_copy(piece, side):
        return pltpu.make_async_copy(
            piece, columns_ref.at[pl.ds(side * half, half)], arrived.at[side]
        )

    def out_copy(n, i):
        slot = i % DEPTH
        return pltpu.make_async_copy(
            made_ref.at[slot, n, pl.ds(0, tiles[i][1])],
            (cov_zero_ref, cov_late_ref)[n].at[pl.ds(*tiles[i]), pl.ds(first, width)],
            stored.at[slot, n],
        )

    for kind, sides in enumerate(PICKS):
        for side, places in enumerate(sides):
            for place, m in enumerate(places):

                @pl.when((place_ref[0] == place) & (place_ref[1] == kind))
                def _():
                    piece_copy(pieces[m], side).start()

    for side in range(2):
        piece_copy(pieces[0], side).wait()
    for i, (top, tile) in enumerate(tiles):
        if i == 0:
            means = dot(masks_ref[...], columns_ref[...]) * scale
        row_mean = mean_ref[top : top + tile, :1]
        for n in range(2):
            if i >= DEPTH:
                out_copy(n, i - DEPTH).wait()
            total = dot((zero_ref, late_ref)[n][top : top + tile], columns_ref[...])
            made_ref[i % DEPTH, n, :tile] = total * scale - row_mean * means[8 * n : 8 * n + 1]
            out_copy(n, i).start()
    for i in range(max(0, len(tiles) - DEPTH), len(tiles)):
        for n in range(2):
            out_copy(n, i).wait()


def product(part, place, count, masks, rows, pieces, before):
    zero, late, means = rows
    height, depth = zero.shape
    width = pieces[0].shape[-1]
    tiles, top = [], 0
    for tile in TILES:
        tile = min(tile, height - top)
        tiles.append((top, tile))
        top += tile
    tile = max(TILES)
    out = jax.ShapeDtypeStruct((height, 2 * width), jnp.float32)
    anywhere = pl.BlockSpec(memory_space=pl.ANY)
    return pl.pallas_call(
        functools.partial(product_kernel, n_pieces=len(pieces), tiles=tiles),
        out_shape=(out, out),
        in_specs=[pl.BlockSpec(memory_space=pltpu.SMEM)] * 3
        + [pl.BlockSpec(memory_space=pltpu.VMEM)] * 4
        + [pl.BlockSpec(memory_space=pltpu.HBM)]
        + [anywhere] * (len(pieces) - 1 + len(before)),
        out_specs=[anywhere] * 2,
        scratch_shapes=[
            pltpu.VMEM((depth, width), jnp.bfloat16),
            pltpu.VMEM((DEPTH, 2, tile, width), jnp.float32),
            pltpu.SemaphoreType.DMA((2,)),
            pltpu.SemaphoreType.DMA((DEPTH, 2)),
        ],
        input_output_aliases={7 + len(pieces) + i: i for i in range(len(before))},
        compiler_params=pltpu.CompilerParams(vmem_limit_bytes=VMEM_LIMIT),
        cost_estimate=pl.CostEstimate(
            flops=4 * height * depth * width,
            bytes_accessed=4 * height * depth + 8 * height * width,
            transcendentals=0,
        ),
        name="covariances",
    )(part, place, count, masks, means, zero, late, *pieces, *before)


def line_of_four(frames, window_starts, lag_frames):
    trajectories, half, features = frames.shape
    stored = 2 * half
    window = stored - SLACK
    z, x, c = (lax.axis_index(a) for a in AXES)
    s = jnp.where(x == 1, 3 - z, z)
    count = (trajectories * window - jnp.sum(lag_frames)).astype(jnp.float32).reshape(1)
    plane = x.astype(jnp.int32).reshape(1)
    part = c.astype(jnp.int32).reshape(1)

    base_mask, lag_mask = window_masks(window_starts, lag_frames, stored)

    def relative(mask):
        low, high = mask[:, :half].reshape(-1), mask[:, half:].reshape(-1)
        return jnp.where(x == 0, jnp.concatenate([low, high]), jnp.concatenate([high, low]))

    masks = jnp.concatenate(
        [
            jnp.broadcast_to(relative(m)[None, :], (8, trajectories * stored))
            for m in (base_mask, lag_mask)
        ]
    )

    picks = jnp.array([[[0, 2, 3, 4], [1, 3, 4, 5]], [[5, 0, 2, 3], [3, 1, 5, 6]]], jnp.int32)
    pick = picks[jnp.where(c == x, 0, 1), :, s]

    place = jnp.stack([s, jnp.where(c == x, 0, 1)]).astype(jnp.int32)
    own = frames
    near1_a, far1_a = send(own, NEAR_1), send(own, FAR_1)
    cross = send(own, PLANES)
    sib = send(own, CORES)
    near1_b, far1_b = send(sib, NEAR_1), send(sib, FAR_1)
    near1_a, far1_a, masks, count, place = lax.optimization_barrier(
        (near1_a, far1_a, masks, count, place)
    )
    near2_a, far2_a = send(jnp.where(s == 0, cross, near1_a), NEAR_2), send(far1_a, FAR_2)
    sib_cross = send(cross, CORES)
    near2_b, far2_b = send(jnp.where(s == 0, sib_cross, near1_b), NEAR_2), send(far1_b, FAR_2)
    near3_a, back_a, close_a = send(near2_a, NEAR_3), send(far2_a, BACK_3), send(after(own, near2_a, far2_a), OWN_3)
    rows = prepare_rows(
        part, window_starts, lag_frames, plane, count, ((own, cross), (sib, sib_cross)), window
    )
    near2_b, far2_b, *rows = lax.optimization_barrier((near2_b, far2_b, *rows))
    near3_b, back_b, close_b = send(near2_b, NEAR_3), send(far2_b, BACK_3), send(after(sib, near2_b, far2_b), OWN_3)

    outs = ()
    for where_to, pieces in (
        (part, (own, cross, near1_a, near2_a, near3_a, back_a, far2_a, close_a)),
        (1 - part, (sib, sib_cross, near1_b, near2_b, near3_b, back_b, far2_b, close_b)),
    ):
        pieces = [piece.reshape(trajectories * half, features) for piece in pieces]
        outs = product(where_to, place, count, masks, rows, pieces, outs)
    return outs


def solution(mesh):
    placed = (P("groups", "tm", ("feat", "sub")), P("groups"), P("groups"))
    line = mesh.shape["feat"] == 4 and mesh.shape["tm"] == 2 and mesh.shape["sub"] == 2
    return jax.shard_map(
        line_of_four if line else general,
        mesh=mesh,
        in_specs=placed,
        out_specs=(P(("groups", "feat"), ("tm", "sub")), P(("groups", "feat"), ("tm", "sub"))),
        check_vma=False,
    )
```

```python
import functools

import jax
import jax.numpy as jnp
from jax import lax
from jax.experimental import pallas as pl
from jax.experimental.pallas import tpu as pltpu
from jax.sharding import PartitionSpec as P

SLACK = 32
LAGMAX = 64
AXES = ("feat", "tm", "sub")
VMEM_LIMIT = 32 * 1024 * 1024
TILES = (1024, 768, 256)
DEPTH = 2
ROWS_TILE = 1024


def spread(x, axis, root):
    mine = lax.axis_index(axis) == root
    return lax.psum(jnp.where(mine, x, jnp.zeros_like(x)), axis)


def window_masks(window_starts, lag_frames, stored):
    instant = jnp.arange(stored, dtype=jnp.int32)[None, :]
    window_begin = window_starts[:, None]
    shift_by = lag_frames[:, None]
    finish = window_begin + (stored - SLACK)
    base_mask = (instant >= window_begin) & (instant < finish - shift_by)
    lag_mask = (instant >= window_begin + shift_by) & (instant < finish)
    return (base_mask.astype(jnp.bfloat16), lag_mask.astype(jnp.bfloat16))


def shift_ahead(series, lag_frames):
    stored = series.shape[1]
    padded = jnp.pad(series, ((0, 0), (0, LAGMAX), (0, 0)))

    def one_series(padded_rows, shift_by):
        return lax.dynamic_slice_in_dim(padded_rows, shift_by, stored, 0)

    return jax.vmap(one_series)(padded, lag_frames)


def frame_product(left, right):
    return lax.dot_general(
        left, right, (((0, 1), (0, 1)), ((), ())), preferred_element_type=jnp.float32
    )


def frame_mean(mask, series, frame_count):
    return jnp.einsum("kt,ktf->f", mask, series, preferred_element_type=jnp.float32) / frame_count


def general(frames, window_starts, lag_frames):
    halves = lax.all_gather(frames, "sub", axis=2, tiled=True)
    row_data = lax.all_gather(halves, "tm", axis=1, tiled=True)
    stored = row_data.shape[1]
    base_mask, lag_mask = window_masks(window_starts, lag_frames, stored)
    frame_count = (row_data.shape[0] * (stored - SLACK) - jnp.sum(lag_frames)).astype(jnp.float32)
    masked_rows = row_data * base_mask[:, :, None]
    row_mean = frame_mean(base_mask, row_data, frame_count)
    groups = lax.axis_size("tm") * lax.axis_size("sub")
    per_group = lax.axis_size("feat") // groups
    column = lax.axis_index("tm") * lax.axis_size("sub") + lax.axis_index("sub")
    tile_parts = []
    for member in range(per_group):
        column_block = spread(row_data, "feat", column * per_group + member)
        zero_mean = frame_mean(base_mask, column_block, frame_count)
        later_mean = frame_mean(lag_mask, column_block, frame_count)
        zero_part = (
            frame_product(masked_rows, column_block) / frame_count
            - row_mean[:, None] * zero_mean[None, :]
        )
        crossed = frame_product(masked_rows, shift_ahead(column_block, lag_frames))
        lag_part = crossed / frame_count - row_mean[:, None] * later_mean[None, :]
        tile_parts.append((zero_part, lag_part))
    covariance_zero = jnp.concatenate([entries[0] for entries in tile_parts], axis=1)
    covariance_lag = jnp.concatenate([entries[1] for entries in tile_parts], axis=1)
    return (covariance_zero, covariance_lag)


def rank(s, x, c):
    return ((3 - s if x else s) * 2 + x) * 2 + c


def home(s, x):
    return (3 - s if x else s) % 2


def hops(links):
    pairs = []
    for s, d, b in links:
        for x in range(2):
            to = rank(d, x, home(b, x)) if d >= 0 else rank(3 - s, 1 - x, home(b, x))
            pairs.append((rank(s, x, home(b, x)), to))
    return pairs


PLACES = [(s, x) for s in range(4) for x in range(2)]
CORES = [(rank(s, x, c), rank(s, x, 1 - c)) for s, x in PLACES for c in range(2)]
PLANES = [(rank(s, x, c), rank(3 - s, 1 - x, c)) for s, x in PLACES for c in range(2)]
NEAR_1 = hops([(0, 1, 0), (1, 2, 1), (2, 3, 2)])
FAR_1 = hops([(3, 2, 3), (2, 0, 2)])
NEAR_2 = hops([(0, 1, 0), (1, 2, 0), (2, 3, 1), (3, -1, 2)])
FAR_2 = hops([(2, 0, 3), (0, -1, 2)])
NEAR_3 = hops([(1, 2, 0), (2, 3, 0)])
BACK_3 = hops([(3, 2, 1), (0, -1, 3)])
OWN_3 = hops([(1, 0, 1)])
PICKS = (((0, 2, 3, 4), (1, 3, 4, 5)), ((7, 0, 2, 3), (3, 1, 5, 6)))


def send(x, pairs):
    return lax.ppermute(x, AXES, pairs)


def after(value, *others):
    return lax.optimization_barrier((value, *others))[0]


def dot(left, right):
    return jnp.dot(left, right, preferred_element_type=jnp.float32)


def rows_kernel(
    starts_ref, lags_ref, x_ref, count_ref, parts, zero_ref, late_ref, mean_ref, moves_ref, *, window
):
    trajectories, half = parts[0][0].shape[0], parts[0][0].shape[1]
    stored = 2 * half
    p, i = pl.program_id(0), pl.program_id(1)

    @pl.when((p == 0) & (i == 0))
    def _():
        def instant(axis):
            n = lax.broadcasted_iota(jnp.int32, (stored, stored), axis)
            return jnp.where(x_ref[0] == 0, n, lax.rem(n + half, stored))

        frame, column = instant(0), instant(1)
        for k in range(trajectories):
            start, lag = starts_ref[k], lags_ref[k]
            kept = (frame >= start) & (frame < start + window - lag)
            for n, ahead in enumerate((0, lag)):
                moves_ref[k, :, n * stored : (n + 1) * stored] = jnp.where(
                    kept & (column == frame + ahead), 1.0, 0.0
                ).astype(jnp.bfloat16)

    def fill(own_ref, cross_ref):
        total = None
        for k in range(trajectories):
            series = jnp.concatenate([own_ref[k], cross_ref[k]], axis=0)
            moved = lax.dot_general(
                series,
                moves_ref[k],
                (((0,), (0,)), ((), ())),
                preferred_element_type=jnp.float32,
            )
            total = moved[:, :stored] if total is None else total + moved[:, :stored]
            moved = moved.astype(jnp.bfloat16)
            for n, ref in enumerate((zero_ref, late_ref)):
                for side in range(2):
                    to, at = (side * trajectories + k) * half, n * stored + side * half
                    ref[:, to : to + half] = moved[:, at : at + half]
        mean = jnp.sum(total, axis=1, keepdims=True) / count_ref[0]
        mean_ref[...] = jnp.broadcast_to(mean, mean_ref.shape)

    for n, (own_ref, cross_ref) in enumerate(parts):
        pl.when(p == n)(functools.partial(fill, own_ref, cross_ref))


def prepare_rows(part, starts, lags, x, count, arrays, window):
    trajectories, half, features = arrays[0][0].shape
    tile = min(ROWS_TILE, features)
    steps = features // tile
    depth = trajectories * 2 * half
    row = jax.ShapeDtypeStruct((2 * features, depth), jnp.bfloat16)
    mean = jax.ShapeDtypeStruct((2 * features, 128), jnp.float32)

    def spot(p, i, part_ref, *_):
        return (jnp.where(p == 0, part_ref[0], 1 - part_ref[0]) * steps + i, 0)

    shape = (trajectories, half, tile)
    first = pl.BlockSpec(shape, lambda p, i, *_: (0, 0, jnp.where(p == 0, i, steps - 1)))
    second = pl.BlockSpec(shape, lambda p, i, *_: (0, 0, jnp.where(p == 0, 0, i)))

    def body(part_ref, starts_ref, lags_ref, x_ref, count_ref, *refs):
        rows_kernel(
            starts_ref, lags_ref, x_ref, count_ref, (refs[:2], refs[2:4]), *refs[4:], window=window
        )

    return pl.pallas_call(
        body,
        out_shape=(row, row, mean),
        grid_spec=pltpu.PrefetchScalarGridSpec(
            num_scalar_prefetch=5,
            grid=(2, steps),
            in_specs=[first] * 2 + [second] * 2,
            out_specs=[
                pl.BlockSpec((tile, depth), spot),
                pl.BlockSpec((tile, depth), spot),
                pl.BlockSpec((tile, 128), spot),
            ],
            scratch_shapes=[pltpu.VMEM((trajectories, 2 * half, 4 * half), jnp.bfloat16)],
        ),
        compiler_params=pltpu.CompilerParams(vmem_limit_bytes=VMEM_LIMIT),
        cost_estimate=pl.CostEstimate(
            flops=0, bytes_accessed=28 * arrays[0][0].size, transcendentals=0
        ),
        name="rows",
    )(part, starts, lags, x, count, *arrays[0], *arrays[1])


def product_kernel(part_ref, place_ref, count_ref, masks_ref, mean_ref, zero_ref, late_ref, *refs, n_pieces, tiles):
    pieces = refs[:n_pieces]
    cov_zero_ref, cov_late_ref, columns_ref, made_ref, arrived, stored = refs[-6:]
    half, width = columns_ref.shape[0] // 2, columns_ref.shape[1]
    scale = 1.0 / count_ref[0]
    first = pl.multiple_of(part_ref[0] * width, width)

    def piece_copy(piece, side):
        return pltpu.make_async_copy(
            piece, columns_ref.at[pl.ds(side * half, half)], arrived.at[side]
        )

    def out_copy(n, i):
        slot = i % DEPTH
        return pltpu.make_async_copy(
            made_ref.at[slot, n, pl.ds(0, tiles[i][1])],
            (cov_zero_ref, cov_late_ref)[n].at[pl.ds(*tiles[i]), pl.ds(first, width)],
            stored.at[slot, n],
        )

    for kind, sides in enumerate(PICKS):
        for side, places in enumerate(sides):
            for place, m in enumerate(places):

                @pl.when((place_ref[0] == place) & (place_ref[1] == kind))
                def _():
                    piece_copy(pieces[m], side).start()

    for side in range(2):
        piece_copy(pieces[0], side).wait()
    for i, (top, tile) in enumerate(tiles):
        if i == 0:
            means = dot(masks_ref[...], columns_ref[...]) * scale
        row_mean = mean_ref[top : top + tile, :1]
        for n in range(2):
            if i >= DEPTH:
                out_copy(n, i - DEPTH).wait()
            total = dot((zero_ref, late_ref)[n][top : top + tile], columns_ref[...])
            made_ref[i % DEPTH, n, :tile] = total * scale - row_mean * means[8 * n : 8 * n + 1]
            out_copy(n, i).start()
    for i in range(max(0, len(tiles) - DEPTH), len(tiles)):
        for n in range(2):
            out_copy(n, i).wait()


def product(part, place, count, masks, rows, pieces, before):
    zero, late, means = rows
    height, depth = zero.shape
    width = pieces[0].shape[-1]
    tiles, top = [], 0
    for tile in TILES:
        tile = min(tile, height - top)
        tiles.append((top, tile))
        top += tile
    tile = max(TILES)
    out = jax.ShapeDtypeStruct((height, 2 * width), jnp.float32)
    anywhere = pl.BlockSpec(memory_space=pl.ANY)
    return pl.pallas_call(
        functools.partial(product_kernel, n_pieces=len(pieces), tiles=tiles),
        out_shape=(out, out),
        in_specs=[pl.BlockSpec(memory_space=pltpu.SMEM)] * 3
        + [pl.BlockSpec(memory_space=pltpu.VMEM)] * 4
        + [anywhere] * (len(pieces) + len(before)),
        out_specs=[anywhere] * 2,
        scratch_shapes=[
            pltpu.VMEM((depth, width), jnp.bfloat16),
            pltpu.VMEM((DEPTH, 2, tile, width), jnp.float32),
            pltpu.SemaphoreType.DMA((2,)),
            pltpu.SemaphoreType.DMA((DEPTH, 2)),
        ],
        input_output_aliases={7 + len(pieces) + i: i for i in range(len(before))},
        compiler_params=pltpu.CompilerParams(vmem_limit_bytes=VMEM_LIMIT),
        cost_estimate=pl.CostEstimate(
            flops=4 * height * depth * width,
            bytes_accessed=4 * height * depth + 8 * height * width,
            transcendentals=0,
        ),
        name="covariances",
    )(part, place, count, masks, means, zero, late, *pieces, *before)


def line_of_four(frames, window_starts, lag_frames):
    trajectories, half, features = frames.shape
    stored = 2 * half
    window = stored - SLACK
    z, x, c = (lax.axis_index(a) for a in AXES)
    s = jnp.where(x == 1, 3 - z, z)
    count = (trajectories * window - jnp.sum(lag_frames)).astype(jnp.float32).reshape(1)
    plane = x.astype(jnp.int32).reshape(1)
    part = c.astype(jnp.int32).reshape(1)

    base_mask, lag_mask = window_masks(window_starts, lag_frames, stored)

    def relative(mask):
        low, high = mask[:, :half].reshape(-1), mask[:, half:].reshape(-1)
        return jnp.where(x == 0, jnp.concatenate([low, high]), jnp.concatenate([high, low]))

    masks = jnp.concatenate(
        [
            jnp.broadcast_to(relative(m)[None, :], (8, trajectories * stored))
            for m in (base_mask, lag_mask)
        ]
    )

    picks = jnp.array([[[0, 2, 3, 4], [1, 3, 4, 5]], [[5, 0, 2, 3], [3, 1, 5, 6]]], jnp.int32)
    pick = picks[jnp.where(c == x, 0, 1), :, s]

    place = jnp.stack([s, jnp.where(c == x, 0, 1)]).astype(jnp.int32)
    own = frames
    near1_a, far1_a = send(own, NEAR_1), send(own, FAR_1)
    cross = send(own, PLANES)
    sib = send(own, CORES)
    near1_b, far1_b = send(sib, NEAR_1), send(sib, FAR_1)
    kept = jnp.where(s < 0, jnp.zeros_like(own), own)
    near1_a, far1_a, masks, count, place, kept = lax.optimization_barrier(
        (near1_a, far1_a, masks, count, place, kept)
    )
    near2_a, far2_a = send(jnp.where(s == 0, cross, near1_a), NEAR_2), send(far1_a, FAR_2)
    sib_cross = send(cross, CORES)
    near2_b, far2_b = send(jnp.where(s == 0, sib_cross, near1_b), NEAR_2), send(far1_b, FAR_2)
    near3_a, back_a, close_a = send(near2_a, NEAR_3), send(far2_a, BACK_3), send(after(own, near2_a, far2_a), OWN_3)
    rows = prepare_rows(
        part, window_starts, lag_frames, plane, count, ((kept, cross), (sib, sib_cross)), window
    )
    near2_b, far2_b, *rows = lax.optimization_barrier((near2_b, far2_b, *rows))
    near3_b, back_b, close_b = send(near2_b, NEAR_3), send(far2_b, BACK_3), send(after(sib, near2_b, far2_b), OWN_3)

    outs = ()
    for where_to, pieces in (
        (part, (kept, cross, near1_a, near2_a, near3_a, back_a, far2_a, close_a)),
        (1 - part, (sib, sib_cross, near1_b, near2_b, near3_b, back_b, far2_b, close_b)),
    ):
        pieces = [piece.reshape(trajectories * half, features) for piece in pieces]
        outs = product(where_to, place, count, masks, rows, pieces, outs)
    return outs


def solution(mesh):
    placed = (P("groups", "tm", ("feat", "sub")), P("groups"), P("groups"))
    line = mesh.shape["feat"] == 4 and mesh.shape["tm"] == 2 and mesh.shape["sub"] == 2
    return jax.shard_map(
        line_of_four if line else general,
        mesh=mesh,
        in_specs=placed,
        out_specs=(P(("groups", "feat"), ("tm", "sub")), P(("groups", "feat"), ("tm", "sub"))),
        check_vma=False,
    )
```
